32 devices in a mesh: dom: 16 (over z, y, x), dim: 2 (over core).
Axes of the slice: x: 2, y: 2, z: 4, core: 2. Of those that a mesh axis runs over, the one named last changes fastest.
Arguments:
- ent_re: float32 [200, 8192], P('dim', 'dom'), may hold values from -8 to 8
- ent_im: float32 [200, 8192], P('dim', 'dom'), may hold values from -8 to 8
- ent_acc: float32 [8192], P('dom'), may hold values from 0.001 to 0.1
- rel_re: float32 [200, 4096], P('dim'), may hold values from -2.5 to 2.5
- rel_im: float32 [200, 4096], P('dim'), may hold values from -2.5 to 2.5
- rel_acc: float32 [4096], replicated, may hold values from 0.001 to 0.1
- lhs_rows: int32 [32, 128], P('dom'), may hold values from 0 to 511
- rhs_rows: int32 [32, 128], P('dom'), may hold values from 0 to 511
- rel_ids: int32 [32, 128], P('dom'), may hold values from 0 to 4095
- neg_rows: int32 [32, 1000], P('dom'), may hold values from 0 to 511
- bucket_step: int32 [32], P('dom'), may hold values from 0 to 4
Outputs:
- new_ent_re: float32 [200, 8192], P('dim', 'dom')
- new_ent_im: float32 [200, 8192], P('dim', 'dom')
- new_ent_acc: float32 [8192], P('dom')
- new_rel_re: float32 [200, 4096], P('dim')
- new_rel_im: float32 [200, 4096], P('dim')
- new_rel_acc: float32 [4096], replicated
The draws below stay inside these ranges and needn't reach their ends.
Inputs may be any that keep to these rules, and one draw needn't show every extreme that they name: bucket_step equal to 4 marks an empty slot.
All inputs are finite; a program needn't handle non-finite values.
Results may differ from the reference program's by a relative error of at most 0.0003.
Values sent between devices are 32-bit elements; how exact they have to be, the bound alone decides.
A program may use at most 64 MiB of HBM per device.

```python
import math
import jax
import jax.numpy as jnp
import numpy as np
from jax import lax

D = 400
HALF = 200
REL = 4096
NEG = 1000
CH = 128
ROWS = 512
GROUPS = 2
STEPS = 4
ENTS = 8192
SLOTS = 32


def entity_values(key):
    base = jnp.clip(jax.random.normal(key, (HALF, ENTS), jnp.float32), -4.0, 4.0)
    return base * 0.5


def draw_ent_re(key, part):
    key = jax.random.fold_in(key, 11)
    return entity_values(key)


def draw_ent_im(key, part):
    key = jax.random.fold_in(key, 23)
    return entity_values(key)


def place_ends(entries, key, smallest, high):
    place = [jax.random.randint(jax.random.fold_in(key, axis), (), 0, length) for axis, length in enumerate(entries.shape)]
    longest = entries.shape.index(max(entries.shape))
    beside = place[:longest] + [(place[longest] + 1) % entries.shape[longest]] + place[longest + 1:]
    return entries.at[tuple(place)].set(smallest).at[tuple(beside)].set(high)


def level_of(own_key, shape, pieces, low, largest):
    gain, own = 1.0, jax.random.fold_in(own_key, 6)
    for dim, shards_of in pieces:
        draws = jnp.exp(jax.random.uniform(jax.random.fold_in(own, dim), (shards_of,), jnp.float32, low / len(pieces), largest / len(pieces)))
        gain = gain * jnp.repeat(draws, shape[dim] // shards_of).reshape([-1 if axis == dim else 1 for axis in range(len(shape))])
    return gain


def cumulative_ranks(number_of, slope):
    weights = [(1 << 20) // math.isqrt(standing ** slope) + 1 for standing in range(1, number_of + 1)]
    deviation = 1 + sum(weights) // (1 << 30)
    return np.cumsum(np.array([max(1, weight // deviation) for weight in weights]))


def ranked(key, extent, number_of, skew):
    listing = cumulative_ranks(number_of, skew)
    ticket = jax.random.randint(jax.random.fold_in(key, 1), extent, 0, int(listing[number_of - 1]))
    rank = jnp.searchsorted(jnp.asarray(listing, jnp.int32), ticket, side="right")
    return jax.random.permutation(jax.random.fold_in(key, 2), number_of)[rank].astype(jnp.int32)


def bell_draw(own_key, shape, deviation, reach, pieces=(), held_as=jnp.bfloat16):
    values = jax.random.normal(own_key, shape, jnp.float32) * deviation
    if len(pieces) > 0:
        values = level_of(own_key, shape, pieces, -0.22, 0.18) * values
    return jnp.clip(values, min=-reach, max=reach).astype(held_as)


def setup_inputs(seed: int = 0) -> dict:
    key_list = jax.random.split(jax.random.key(seed), 12)
    ent_re = draw_ent_re(jax.random.fold_in(key_list[11], 71), 0)
    ent_im = draw_ent_im(jax.random.fold_in(key_list[11], 71), 0)
    ent_acc = jnp.clip(jnp.exp(math.log(0.1) - 4.6051702 * jax.random.uniform(key_list[2], (ENTS,), jnp.float32) ** level_of(key_list[2], (ENTS,), ((0, 16),), -0.2, 0.2)), 0.001, 0.1)
    rel_re = bell_draw(key_list[3], (HALF, REL), 0.42, 2.5, ((0, 2),), jnp.float32)
    rel_im = bell_draw(key_list[4], (HALF, REL), 0.42, 2.5, ((0, 2),), jnp.float32)
    rel_acc = jnp.clip(jnp.exp(jax.random.uniform(key_list[5], (REL,), jnp.float32, math.log(0.001), math.log(0.1))), 0.001, 0.1)
    lhs_rows = place_ends(jax.random.randint(key_list[6], (SLOTS, CH), 0, ROWS), jax.random.fold_in(key_list[6], 1), 0, ROWS - 1).astype(jnp.int32)
    rhs_rows = place_ends(jax.random.randint(key_list[7], (SLOTS, CH), 0, ROWS), jax.random.fold_in(key_list[7], 1), 0, ROWS - 1).astype(jnp.int32)
    rel_ids = place_ends(ranked(key_list[8], (SLOTS, CH), REL, 2), jax.random.fold_in(key_list[8], 3), 0, REL - 1).astype(jnp.int32)
    neg_rows = place_ends(jax.random.randint(key_list[9], (SLOTS, NEG), 0, ROWS), jax.random.fold_in(key_list[9], 1), 0, ROWS - 1).astype(jnp.int32)
    bucket_step = place_ends(ranked(key_list[10], (SLOTS,), STEPS + 1, 2), jax.random.fold_in(key_list[10], 3), 0, STEPS).astype(jnp.int32)
    return dict(ent_re=ent_re, ent_im=ent_im, ent_acc=ent_acc, rel_re=rel_re, rel_im=rel_im, rel_acc=rel_acc, lhs_rows=lhs_rows, rhs_rows=rhs_rows, rel_ids=rel_ids, neg_rows=neg_rows, bucket_step=bucket_step)


learn_rate = 0.1

def reference(ent_re, ent_im, ent_acc, rel_re, rel_im, rel_acc, lhs_rows, rhs_rows, rel_ids, neg_rows, bucket_step):
    ent_re = ent_re.T
    ent_im = ent_im.T
    rel_re = rel_re.T
    rel_im = rel_im.T
    parts = ENTS // ROWS
    holder = jnp.arange(SLOTS, dtype=jnp.int32) // GROUPS
    live = (bucket_step < STEPS).astype(jnp.float32)
    stepc = jnp.minimum(bucket_step, STEPS - 1).astype(jnp.int32)
    target = (holder - stepc) % parts
    lhs_glob = lhs_rows + (holder * ROWS)[:, None]
    rhs_glob = rhs_rows + (target * ROWS)[:, None]
    neg_glob = neg_rows + (target * ROWS)[:, None]
    h_re, h_im = (ent_re[lhs_glob], ent_im[lhs_glob])
    r_re, r_im = (rel_re[rel_ids], rel_im[rel_ids])
    t_re, t_im = (ent_re[rhs_glob], ent_im[rhs_glob])
    n_re, n_im = (ent_re[neg_glob], ent_im[neg_glob])
    q_re = h_re * r_re - h_im * r_im
    q_im = h_re * r_im + h_im * r_re
    hp = lax.Precision.HIGHEST
    pos = lax.optimization_barrier(jnp.sum(q_re * t_re + q_im * t_im, -1))
    neg = jnp.einsum('cek,cnk->cen', q_re, n_re, precision=hp) + jnp.einsum('cek,cnk->cen', q_im, n_im, precision=hp)
    top = jnp.maximum(lax.optimization_barrier(jnp.max(neg, -1)), pos)
    e_pos = jnp.exp(pos - top)
    e_neg = jnp.exp(neg - top[..., None])
    denom = e_pos + lax.optimization_barrier(jnp.sum(e_neg, -1))
    w_pos = (e_pos / denom - 1.0) * live[:, None]
    w_neg = e_neg / denom[..., None] * live[:, None, None]
    gq_re = w_pos[..., None] * t_re + jnp.einsum('cen,cnk->cek', w_neg, n_re, precision=hp)
    gq_im = w_pos[..., None] * t_im + jnp.einsum('cen,cnk->cek', w_neg, n_im, precision=hp)
    gt_re, gt_im = (w_pos[..., None] * q_re, w_pos[..., None] * q_im)
    gn_re = jnp.einsum('cen,cek->cnk', w_neg, q_re, precision=hp)
    gn_im = jnp.einsum('cen,cek->cnk', w_neg, q_im, precision=hp)
    gh_re = gq_re * r_re + gq_im * r_im
    gh_im = gq_im * r_re - gq_re * r_im
    gr_re = gq_re * h_re + gq_im * h_im
    gr_im = gq_im * h_re - gq_re * h_im

    def scatter(values_a, ids_a, values_b, ids_b, values_c, ids_c):
        half = values_a.shape[-1]
        total = jax.ops.segment_sum(values_a.reshape(-1, half), ids_a.reshape(-1), ENTS)
        total = total + jax.ops.segment_sum(values_b.reshape(-1, half), ids_b.reshape(-1), ENTS)
        return total + jax.ops.segment_sum(values_c.reshape(-1, half), ids_c.reshape(-1), ENTS)
    g_re = scatter(gh_re, lhs_glob, gt_re, rhs_glob, gn_re, neg_glob)
    g_im = scatter(gh_im, lhs_glob, gt_im, rhs_glob, gn_im, neg_glob)
    rg_re = jax.ops.segment_sum(gr_re.reshape(-1, HALF), rel_ids.reshape(-1), REL)
    rg_im = jax.ops.segment_sum(gr_im.reshape(-1, HALF), rel_ids.reshape(-1), REL)
    new_ent_acc = ent_acc + lax.optimization_barrier(jnp.sum(g_re * g_re + g_im * g_im, -1)) / D
    new_rel_acc = rel_acc + lax.optimization_barrier(jnp.sum(rg_re * rg_re + rg_im * rg_im, -1)) / D
    ent_scale = learn_rate / jnp.sqrt(new_ent_acc)[:, None]
    rel_scale = learn_rate / jnp.sqrt(new_rel_acc)[:, None]
    return ((ent_re - ent_scale * g_re).T, (ent_im - ent_scale * g_im).T, new_ent_acc, (rel_re - rel_scale * rg_re).T, (rel_im - rel_scale * rg_im).T, new_rel_acc)
```

```python
import functools
import jax
import jax.numpy as jnp
from jax import lax
from jax.experimental import pallas as pl
from jax.experimental.pallas import tpu as pltpu
from jax.sharding import PartitionSpec as P

D = 400
STEPS = 4
RATE = 0.1
MESH = pl.DeviceIdType.MESH
HP = lax.Precision.HIGHEST
F32 = jnp.float32
BF16 = jnp.bfloat16
META = 16
LANES = 128


def split(x, n):
    parts = []
    for _ in range(n):
        part = x.astype(BF16)
        parts.append(part)
        x = x - part.astype(F32)
    return parts


def one_hot(row, first, count):
    rows = lax.broadcasted_iota(jnp.int32, (count, row.shape[1]), 0) + first
    return jnp.where(rows == row, 1.0, 0.0).astype(BF16)


def pick(x, hot, n):
    total = None
    for part in split(x, n):
        term = jnp.dot(part, hot, preferred_element_type=F32)
        total = term if total is None else total + term
    return total


def put(x, hot, n):
    total = None
    for part in split(x, n):
        term = lax.dot_general(part, hot, (((1,), (1,)), ((), ())), preferred_element_type=F32)
        total = term if total is None else total + term
    return total


def when(pred, fn):
    if isinstance(pred, bool):
        if pred:
            fn()
    else:
        pl.when(pred)(fn)


def wait_for(ref, sem):
    pltpu.make_async_copy(ref, ref, sem).wait()


def remote(src, dst, send, recv, device):
    return pltpu.make_async_remote_copy(
        src_ref=src, dst_ref=dst, send_sem=send, recv_sem=recv, device_id=device, device_id_type=MESH
    )


def query_kernel(
    n_dom, n_dim,
    ent_re, ent_im, rel_re, rel_im, lhs_ref, rhs_ref, ids_ref, neg_ref, bs_ref,
    grel, gent,
    qs, qr, mt, mr, bf, gqo, gqr, gbo, gbr, hs, rs,
    q_send, q_recv, m_send, m_recv, b_send, b_recv, g_send, g_recv, e_send, e_recv,
):
    p, d = lax.axis_index("dom"), lax.axis_index("dim")
    width, rows = ent_re.shape
    groups, per_edge = lhs_ref.shape
    rel_count = rel_re.shape[1]
    wp = qs.shape[1] // 2
    kp = 2 * wp
    units = groups * STEPS // n_dim

    def unit(td, i):
        if n_dim == groups:
            return i, td
        number = td + n_dim * i
        return lax.div(number, groups), lax.rem(number, groups)

    def holder(offset):
        return lax.rem(p + offset + n_dom, n_dom)

    def other(o):
        return lax.rem(d + o, n_dim)

    barrier = pltpu.get_barrier_semaphore()
    peers = 0
    for offset in range(1 - STEPS, STEPS):
        for o in range(n_dim):
            if offset != 0 or o != 0:
                pl.semaphore_signal(barrier, inc=1, device_id=(holder(offset), other(o)), device_id_type=MESH)
                peers += 1

    mt[...] = jnp.full(mt.shape, -1, jnp.int32)
    n_neg = neg_ref.shape[1]
    for g in range(groups):
        for j in range(0, n_neg, LANES):
            wide = min(LANES, n_neg - j)
            mt[g, j // LANES : j // LANES + 1, 0:wide] = neg_ref[g : g + 1, j : j + wide]
        mt[g, 8:9, :] = rhs_ref[g : g + 1, :]
        mt[g, 9:10, :] = jnp.broadcast_to(bs_ref[:, g : g + 1], (1, LANES))
    bf[d] = jnp.zeros((kp, rows), F32)
    bf[d, 0:width, :] = ent_re[...]
    bf[d, wp : wp + width, :] = ent_im[...]

    pl.semaphore_wait(barrier, peers)

    for o in range(1, n_dim):
        remote(bf.at[d], bf.at[d], b_send.at[o], b_recv.at[d], (p, other(o))).start()
    for i in range(units):
        s, g = unit(d, i)

        def local_meta(g=g, i=i):
            mr[i] = mt[g]

        def far_meta(s=s, g=g, i=i):
            remote(mt.at[g], mr.at[i], m_send.at[i], m_recv.at[i], (holder(-s), d)).start()

        when(s == 0, local_meta)
        when(s != 0, far_meta)

    lhs = jnp.concatenate([lhs_ref[g : g + 1, :] for g in range(groups)], 1)
    ids = jnp.concatenate([ids_ref[g : g + 1, :] for g in range(groups)], 1)
    hot_lhs = one_hot(lhs, 0, rows)
    h_re, h_im = pick(ent_re[...], hot_lhs, 3), pick(ent_im[...], hot_lhs, 3)
    chunk = 512

    def gather(c, carry):
        first = pl.multiple_of(c * chunk, chunk)
        hot = one_hot(ids, first, chunk)
        return (
            carry[0] + pick(rel_re[:, pl.ds(first, chunk)], hot, 3),
            carry[1] + pick(rel_im[:, pl.ds(first, chunk)], hot, 3),
        )

    empty = jnp.zeros((width, groups * per_edge), F32)
    r_re, r_im = lax.fori_loop(0, rel_count // chunk, gather, (empty, empty))
    hs[0:width, :] = h_re
    hs[wp : wp + width, :] = h_im
    rs[0:width, :] = r_re
    rs[wp : wp + width, :] = r_im
    q_re = h_re * r_re - h_im * r_im
    q_im = h_re * r_im + h_im * r_re
    qs[...] = jnp.zeros(qs.shape, F32)
    for g in range(groups):
        part = slice(g * per_edge, (g + 1) * per_edge)
        qs[g, 0:width, :] = q_re[:, part]
        qs[g, wp : wp + width, :] = q_im[:, part]

    for i in range(units):
        for o in range(n_dim):
            td = other(o)
            s, g = unit(td, i)

            def near_query(g=g, i=i):
                qr[i, d] = qs[g]

            def far_query(s=s, g=g, i=i, o=o, td=td):
                remote(qs.at[g], qr.at[i, d], q_send.at[i, o], q_recv.at[i, d], (holder(-s), td)).start()

            if o == 0:
                when(s == 0, near_query)
                when(s != 0, far_query)
            else:
                far_query()

    for o in range(1, n_dim):
        wait_for(bf.at[other(o)], b_recv.at[other(o)])

    at = lax.broadcasted_iota(jnp.int32, (rows, per_edge), 0)
    ones = jnp.ones((LANES, per_edge), BF16)
    for i in range(units):
        s, g = unit(d, i)
        when(s != 0, lambda i=i: wait_for(mr.at[i], m_recv.at[i]))
        hits = jnp.zeros((rows, LANES), F32)
        for j in range(8):
            hits = hits + jnp.where(at == mr[i, j : j + 1, :], 1.0, 0.0)
        cnt = jnp.dot(hits.astype(BF16), ones, preferred_element_type=F32)
        hit = at == mr[i, 8:9, :]
        live = jnp.where(mr[i, 9:10, :] == s, 1.0, 0.0)
        for o in range(n_dim):
            if o == 0:
                when(s != 0, lambda i=i: wait_for(qr.at[i, d], q_recv.at[i, d]))
            else:
                wait_for(qr.at[i, other(o)], q_recv.at[i, other(o)])
        block = bf[...].reshape(n_dim * kp, rows)
        q = qr[i].reshape(n_dim * kp, per_edge)
        st = lax.dot_general(block, q, (((0,), (0,)), ((), ())), precision=HP, preferred_element_type=F32)
        pos = jnp.sum(jnp.where(hit, st, 0.0), 0, keepdims=True)
        masked = jnp.where(cnt > 0.0, st, -3.0e38)
        top = jnp.maximum(jnp.max(masked, 0, keepdims=True), pos)
        e_neg = cnt * jnp.exp(masked - top)
        e_pos = jnp.exp(pos - top)
        scale = live / (e_pos + jnp.sum(e_neg, 0, keepdims=True))
        w = e_neg * scale + jnp.where(hit, e_pos * scale - live, 0.0)
        gq = jnp.dot(block, w, precision=HP, preferred_element_type=F32)
        gqo[i] = gq.reshape(n_dim, kp, per_edge)
        for o in range(n_dim):
            td = other(o)

            def near_grad(s=s, g=g, i=i):
                gqr[s, g] = gqo[i, d]

            def far_grad(s=s, g=g, i=i, o=o, td=td):
                remote(gqo.at[i, td], gqr.at[s, g], g_send.at[i, o], g_recv.at[s, g], (holder(s), td)).start()

            if o == 0:
                when(s == 0, near_grad)
                when(s != 0, far_grad)
            else:
                far_grad()
        gb = lax.dot_general(q, w, (((1,), (1,)), ((), ())), precision=HP, preferred_element_type=F32)
        gb = gb.reshape(n_dim, kp, rows)
        gbo[...] = gb if i == 0 else gbo[...] + gb
    for o in range(1, n_dim):
        remote(gbo.at[other(o)], gbr.at[d], e_send.at[o], e_recv.at[d], (p, other(o))).start()

    cols = []
    for g in range(groups):
        total = None
        for s in range(STEPS):
            handler = (s * groups + g) % n_dim
            if s == 0:
                when(d != handler, lambda s=s, g=g: wait_for(gqr.at[s, g], g_recv.at[s, g]))
            else:
                wait_for(gqr.at[s, g], g_recv.at[s, g])
            total = gqr[s, g] if total is None else total + gqr[s, g]
        cols.append(total)
    gq = jnp.concatenate(cols, 1)
    gq_re, gq_im = gq[0:width], gq[wp : wp + width]
    h_re, h_im = hs[0:width, :], hs[wp : wp + width, :]
    r_re, r_im = rs[0:width, :], rs[wp : wp + width, :]
    grel[...] = jnp.zeros(grel.shape, F32)
    grel[0:width, :] = gq_re * h_re + gq_im * h_im
    grel[wp : wp + width, :] = gq_im * h_re - gq_re * h_im
    grel[width : width + 1, :] = ids.astype(F32)
    gent[...] = gbo[d]
    for o in range(1, n_dim):
        wait_for(gbr.at[other(o)], e_recv.at[other(o)])
        gent[...] += gbr[other(o)]
    hot_lhs = one_hot(lhs, 0, rows)
    gent[0:width, :] += put(gq_re * r_re + gq_im * r_im, hot_lhs, 2)
    gent[wp : wp + width, :] += put(gq_im * r_re - gq_re * r_im, hot_lhs, 2)

    for o in range(1, n_dim):
        wait_for(bf.at[d], b_send.at[o])
        wait_for(gbo.at[d], e_send.at[o])
    for i in range(units):
        s, g = unit(d, i)
        when(s != 0, lambda i=i: wait_for(mt.at[0], m_send.at[i]))
        when(s != 0, lambda i=i: wait_for(qs.at[0], q_send.at[i, 0]))
        when(s != 0, lambda i=i: wait_for(gqo.at[i, 0], g_send.at[i, 0]))
        for o in range(1, n_dim):
            wait_for(qs.at[0], q_send.at[i, o])
            wait_for(gqo.at[i, 0], g_send.at[i, o])


def relation_kernel(
    n_dom, n_dim,
    grel, gent, ent_re, ent_im, ent_acc, rel_re, rel_im, rel_acc,
    new_re, new_im, new_acc, new_rre, new_rim, new_racc,
    slots, acc, esq, rsq,
    send, recv, eq_send, eq_recv, rq_send, rq_recv,
):
    p, d = lax.axis_index("dom"), lax.axis_index("dim")
    width = ent_re.shape[0]
    wp = grel.shape[0] // 2
    edges = grel.shape[1]
    rel_count = rel_re.shape[1]
    deep = n_dom // 4
    z, y, x = lax.div(p, 4), lax.rem(lax.div(p, 2), 2), lax.rem(p, 2)

    def index(zz, yy, xx):
        return zz * 4 + yy * 2 + xx

    def other(o):
        return lax.rem(d + o, n_dim)

    to_x, to_y = index(z, y, 1 - x), index(z, 1 - y, x)
    up, down = p + 4, p - 4
    has_up, has_down = z < deep - 1, z > 0

    barrier = pltpu.get_barrier_semaphore()
    for o in range(1, n_dim):
        pl.semaphore_signal(barrier, inc=1, device_id=(p, other(o)), device_id_type=MESH)
    for q in (to_x, to_y):
        pl.semaphore_signal(barrier, inc=1, device_id=(q, d), device_id_type=MESH)

    @pl.when(has_up)
    def _():
        pl.semaphore_signal(barrier, inc=1, device_id=(up, d), device_id_type=MESH)

    @pl.when(has_down)
    def _():
        pl.semaphore_signal(barrier, inc=1, device_id=(down, d), device_id_type=MESH)

    slots[p, 0] = grel[0:wp, :]
    slots[p, 1] = grel[wp : 2 * wp, :]
    pl.semaphore_wait(barrier, 1 + n_dim + jnp.minimum(z, 1) + jnp.minimum(deep - 1 - z, 1))

    def pass_on(j, half, way, target):
        remote(slots.at[j, half], slots.at[j, half], send.at[j, half, way], recv.at[j, half], (target, d)).start()

    def arrived(j, half):
        wait_for(slots.at[j, half], recv.at[j, half])

    def sent(j, half, way):
        wait_for(slots.at[j, half], send.at[j, half, way])

    def spread(j):
        pass_on(j, 0, 2, to_x)
        pass_on(j, 1, 3, to_y)
        pass_on(j, 0, 3, to_y)
        pass_on(j, 1, 2, to_x)

    def go_up(j):
        @pl.when(has_up)
        def _():
            pass_on(j, 0, 0, up)
            pass_on(j, 1, 0, up)

    def go_down(j):
        @pl.when(has_down)
        def _():
            pass_on(j, 0, 1, down)
            pass_on(j, 1, 1, down)

    go_up(p)
    go_down(p)
    spread(p)

    g_re, g_im = gent[0:width, :], gent[wp : wp + width, :]
    esq[d] = jnp.sum(g_re * g_re, 0, keepdims=True) + jnp.sum(g_im * g_im, 0, keepdims=True)
    for o in range(1, n_dim):
        remote(esq.at[d], esq.at[d], eq_send.at[o], eq_recv.at[d], (p, other(o))).start()

    chunk = 512

    def add_up(j):
        ids = slots[j, 0, width : width + 1, :].astype(jnp.int32)
        parts = split(slots[j].reshape(2 * wp, edges), 2)

        def body(c, carry):
            first = pl.multiple_of(c * chunk, chunk)
            hot = one_hot(ids, first, chunk)
            total = acc[:, pl.ds(first, chunk)]
            for part in parts:
                total = total + lax.dot_general(part, hot, (((1,), (1,)), ((), ())), preferred_element_type=F32)
            acc[:, pl.ds(first, chunk)] = total
            return carry

        lax.fori_loop(0, rel_count // chunk, body, 0)

    acc[...] = jnp.zeros(acc.shape, F32)

    def cross(zz):
        from_x, from_y = index(zz, y, 1 - x), index(zz, 1 - y, x)
        arrived(from_x, 0)
        pass_on(from_x, 0, 3, to_y)
        arrived(from_y, 1)
        pass_on(from_y, 1, 2, to_x)

    def column(k, carry):
        below, above = z - k, z + k

        @pl.when(below >= 0)
        def _():
            j = index(below, y, x)
            arrived(j, 0)
            arrived(j, 1)
            go_up(j)
            spread(j)

        @pl.when(above < deep)
        def _():
            j = index(above, y, x)
            arrived(j, 0)
            arrived(j, 1)
            go_down(j)
            spread(j)

        @pl.when(below + 1 >= 0)
        def _():
            cross(below + 1)
            add_up(index(below + 1, y, x))

        @pl.when((above - 1 < deep) & (k > 1))
        def _():
            cross(above - 1)
            add_up(index(above - 1, y, x))

        return carry

    lax.fori_loop(1, deep, column, 0)
    for far in (z - (deep - 1), z + (deep - 1)):

        @pl.when((far >= 0) & (far < deep))
        def _(far=far):
            cross(far)
            add_up(index(far, y, x))

    total = esq[d]
    for o in range(1, n_dim):
        wait_for(esq.at[other(o)], eq_recv.at[other(o)])
        total = total + esq[other(o)]
    total = ent_acc[...] + total / D
    new_acc[...] = total
    scale = RATE / jnp.sqrt(total)
    new_re[...] = ent_re[...] - scale * gent[0:width, :]
    new_im[...] = ent_im[...] - scale * gent[wp : wp + width, :]

    def rest(zz, carry):
        j = index(zz, y, 1 - x)
        arrived(j, 1)
        add_up(j)
        j = index(zz, 1 - y, x)
        arrived(j, 0)
        add_up(j)
        j = index(zz, 1 - y, 1 - x)
        arrived(j, 0)
        arrived(j, 1)
        add_up(j)
        return carry

    lax.fori_loop(0, deep, rest, 0)

    t_re, t_im = acc[0:width, :], acc[wp : wp + width, :]
    rsq[d] = jnp.sum(t_re * t_re, 0, keepdims=True) + jnp.sum(t_im * t_im, 0, keepdims=True)
    for o in range(1, n_dim):
        remote(rsq.at[d], rsq.at[d], rq_send.at[o], rq_recv.at[d], (p, other(o))).start()
    total = rsq[d]
    for o in range(1, n_dim):
        wait_for(rsq.at[other(o)], rq_recv.at[other(o)])
        total = total + rsq[other(o)]
    total = rel_acc[...] + total / D
    new_racc[...] = total
    scale = RATE / jnp.sqrt(total)
    new_rre[...] = rel_re[...] - scale * acc[0:width, :]
    new_rim[...] = rel_im[...] - scale * acc[wp : wp + width, :]

    def drain(zz, carry):
        j = index(zz, y, x)
        for half in (0, 1):

            @pl.when((zz <= z) & has_up)
            def _(half=half):
                sent(j, half, 0)

            @pl.when((zz >= z) & has_down)
            def _(half=half):
                sent(j, half, 1)

            sent(j, half, 2)
            sent(j, half, 3)
        sent(index(zz, y, 1 - x), 0, 3)
        sent(index(zz, 1 - y, x), 1, 2)
        return carry

    lax.fori_loop(0, deep, drain, 0)
    for o in range(1, n_dim):
        wait_for(esq.at[d], eq_send.at[o])
        wait_for(rsq.at[d], rq_send.at[o])


def per_device(
    n_dom, n_dim,
    ent_re, ent_im, ent_acc, rel_re, rel_im, rel_acc, lhs_rows, rhs_rows, rel_ids, neg_rows, bucket_step,
):
    width, rows = ent_re.shape
    rel_count = rel_re.shape[1]
    groups, per_edge = lhs_rows.shape
    wp = (width // 8 + 1) * 8
    kp = 2 * wp
    units = groups * STEPS // n_dim
    edges = groups * per_edge
    vmem = pl.BlockSpec(memory_space=pltpu.VMEM)
    dma = pltpu.SemaphoreType.DMA
    shape = jax.ShapeDtypeStruct
    grel, gent = pl.pallas_call(
        functools.partial(query_kernel, n_dom, n_dim),
        out_shape=(shape((kp, edges), F32), shape((kp, rows), F32)),
        in_specs=[vmem] * 9,
        out_specs=(vmem, vmem),
        scratch_shapes=[
            pltpu.VMEM((groups, kp, per_edge), F32),
            pltpu.VMEM((units, n_dim, kp, per_edge), F32),
            pltpu.VMEM((groups, META, LANES), jnp.int32),
            pltpu.VMEM((units, META, LANES), jnp.int32),
            pltpu.VMEM((n_dim, kp, rows), F32),
            pltpu.VMEM((units, n_dim, kp, per_edge), F32),
            pltpu.VMEM((STEPS, groups, kp, per_edge), F32),
            pltpu.VMEM((n_dim, kp, rows), F32),
            pltpu.VMEM((n_dim, kp, rows), F32),
            pltpu.VMEM((kp, edges), F32),
            pltpu.VMEM((kp, edges), F32),
            dma((units, n_dim)), dma((units, n_dim)),
            dma((units,)), dma((units,)),
            dma((n_dim,)), dma((n_dim,)),
            dma((units, n_dim)), dma((STEPS, groups)),
            dma((n_dim,)), dma((n_dim,)),
        ],
        compiler_params=pltpu.CompilerParams(
            collective_id=0, has_side_effects=True, vmem_limit_bytes=48 * 1024 * 1024
        ),
    )(ent_re, ent_im, rel_re, rel_im, lhs_rows, rhs_rows, rel_ids, neg_rows, bucket_step.reshape(1, groups))
    outs = pl.pallas_call(
        functools.partial(relation_kernel, n_dom, n_dim),
        out_shape=(
            shape((width, rows), F32), shape((width, rows), F32), shape((1, rows), F32),
            shape((width, rel_count), F32), shape((width, rel_count), F32), shape((1, rel_count), F32),
        ),
        in_specs=[vmem] * 8,
        out_specs=(vmem,) * 6,
        scratch_shapes=[
            pltpu.VMEM((n_dom, 2, wp, edges), F32),
            pltpu.VMEM((kp, rel_count), F32),
            pltpu.VMEM((n_dim, 1, rows), F32),
            pltpu.VMEM((n_dim, 1, rel_count), F32),
            dma((n_dom, 2, 4)), dma((n_dom, 2)),
            dma((n_dim,)), dma((n_dim,)),
            dma((n_dim,)), dma((n_dim,)),
        ],
        compiler_params=pltpu.CompilerParams(
            collective_id=1, has_side_effects=True, vmem_limit_bytes=48 * 1024 * 1024
        ),
    )(
        grel, gent, ent_re, ent_im, ent_acc.reshape(1, rows), rel_re, rel_im, rel_acc.reshape(1, rel_count)
    )
    return outs[0], outs[1], outs[2].reshape(rows), outs[3], outs[4], outs[5].reshape(rel_count)


def solution(mesh):
    return jax.shard_map(
        functools.partial(per_device, mesh.shape["dom"], mesh.shape["dim"]),
        mesh=mesh,
        in_specs=(
            P("dim", "dom"),
            P("dim", "dom"),
            P("dom"),
            P("dim", None),
            P("dim", None),
            P(),
            P("dom", None),
            P("dom", None),
            P("dom", None),
            P("dom", None),
            P("dom"),
        ),
        out_specs=(P("dim", "dom"), P("dim", "dom"), P("dom"), P("dim", None), P("dim", None), P()),
        check_vma=False,
    )
```

```python
import functools
import jax
import jax.numpy as jnp
from jax import lax
from jax.experimental import pallas as pl
from jax.experimental.pallas import tpu as pltpu
from jax.sharding import PartitionSpec as P

D = 400
STEPS = 4
RATE = 0.1
MESH = pl.DeviceIdType.MESH
F32 = jnp.float32
BF16 = jnp.bfloat16
META = 16
LANES = 128


def split(x, n):
    parts = []
    for _ in range(n):
        part = x.astype(BF16)
        parts.append(part)
        x = x - part.astype(F32)
    return parts


def one_hot(row, first, count):
    rows = lax.broadcasted_iota(jnp.int32, (count, row.shape[1]), 0) + first
    return jnp.where(rows == row, 1.0, 0.0).astype(BF16)


def pick(x, hot, n):
    total = None
    for part in split(x, n):
        term = jnp.dot(part, hot, preferred_element_type=F32)
        total = term if total is None else total + term
    return total


def put(x, hot, n):
    total = None
    for part in split(x, n):
        term = lax.dot_general(part, hot, (((1,), (1,)), ((), ())), preferred_element_type=F32)
        total = term if total is None else total + term
    return total


def when(pred, fn):
    if isinstance(pred, bool):
        if pred:
            fn()
    else:
        pl.when(pred)(fn)


def wait_for(ref, sem):
    pltpu.make_async_copy(ref, ref, sem).wait()


def remote(src, dst, send, recv, device):
    return pltpu.make_async_remote_copy(
        src_ref=src, dst_ref=dst, send_sem=send, recv_sem=recv, device_id=device, device_id_type=MESH
    )


def round_kernel(
    n_dom, n_dim,
    ent_re_in, ent_im_in, ent_acc_in, rel_re_in, rel_im_in, rel_acc_in, lhs_in, rhs_in, ids_in, neg_in, bs_in,
    new_re, new_im, new_acc, new_rre, new_rim, new_racc,
    ent_re, ent_im, ent_acc, rel_re, rel_im, rel_acc, lhs_ref, rhs_ref, ids_ref, neg_ref, bs_ref,
    qs, qr, mt, mr, bf, bt, bp, wts, gqo, gqr, gbo, gbr, gent,
    slots, acc, batch, esq, rsq,
    in_sem,
    q_send, q_recv, m_send, m_recv, b_send, b_recv, g_send, g_recv, e_send, e_recv,
    send, recv, eq_send, eq_recv, rq_send, rq_recv,
):
    p, d = lax.axis_index("dom"), lax.axis_index("dim")
    width, rows = ent_re.shape
    groups, per_edge = lhs_ref.shape
    edges = groups * per_edge
    rel_count = rel_re.shape[1]
    kp = qs.shape[1]
    wp = kp // 2
    units = groups * STEPS // n_dim
    deep = n_dom // 4
    z, y, x = lax.div(p, 4), lax.rem(lax.div(p, 2), 2), lax.rem(p, 2)

    def index(zz, yy, xx):
        return zz * 4 + yy * 2 + xx

    def unit(td, i):
        if n_dim == groups:
            return i, td
        number = td + n_dim * i
        return lax.div(number, groups), lax.rem(number, groups)

    def holder(offset):
        return lax.rem(p + offset + n_dom, n_dom)

    def other(o):
        return lax.rem(d + o, n_dim)

    to_x, to_y = index(z, y, 1 - x), index(z, 1 - y, x)
    up, down = p + 4, p - 4
    has_up, has_down = z < deep - 1, z > 0

    barrier = pltpu.get_barrier_semaphore()

    def greet(dom, dim):
        pl.semaphore_signal(barrier, inc=1, device_id=(dom, dim), device_id_type=MESH)

    peers = 0
    for offset in range(1 - STEPS, STEPS):
        for o in range(n_dim):
            if offset != 0 or o != 0:
                greet(holder(offset), other(o))
                peers += 1
    greet(to_x, d)
    greet(to_y, d)

    @pl.when(has_up)
    def _():
        greet(up, d)

    @pl.when(has_down)
    def _():
        greet(down, d)

    fetches = []
    for k, (src, dst) in enumerate([
        (lhs_in, lhs_ref), (rhs_in, rhs_ref), (ids_in, ids_ref), (neg_in, neg_ref), (bs_in, bs_ref),
        (ent_re_in, ent_re), (ent_im_in, ent_im), (rel_re_in, rel_re), (rel_im_in, rel_im),
        (ent_acc_in, ent_acc), (rel_acc_in, rel_acc),
    ]):
        fetches.append(pltpu.make_async_copy(src, dst, in_sem.at[k]))
        fetches[-1].start()
    mt[...] = jnp.full(mt.shape, -1, jnp.int32)
    qs[...] = jnp.zeros(qs.shape, F32)
    for half in (0, 1):
        slots[p, half] = jnp.zeros((wp, edges), F32)
    bf[d] = jnp.zeros((kp, rows), F32)
    for fetch in fetches[:7]:
        fetch.wait()

    n_neg = neg_ref.shape[1]
    for g in range(groups):
        for j in range(0, n_neg, LANES):
            wide = min(LANES, n_neg - j)
            mt[g, j // LANES : j // LANES + 1, 0:wide] = neg_ref[g : g + 1, j : j + wide]
        mt[g, 8:9, :] = rhs_ref[g : g + 1, :]
        mt[g, 9:10, :] = jnp.broadcast_to(bs_ref[:, g : g + 1], (1, LANES))
    bf[d, 0:width, :] = ent_re[...]
    bf[d, wp : wp + width, :] = ent_im[...]

    pl.semaphore_wait(barrier, peers + 2 + jnp.minimum(z, 1) + jnp.minimum(deep - 1 - z, 1))

    for i in range(units):
        s, g = unit(d, i)

        def local_meta(g=g, i=i):
            mr[i] = mt[g]

        def far_meta(s=s, g=g, i=i):
            remote(mt.at[g], mr.at[i], m_send.at[i], m_recv.at[i], (holder(-s), d)).start()

        when(s == 0, local_meta)
        when(s != 0, far_meta)
    for o in range(1, n_dim):
        remote(bf.at[d], bf.at[d], b_send.at[o], b_recv.at[d], (p, other(o))).start()

    lhs = jnp.concatenate([lhs_ref[g : g + 1, :] for g in range(groups)], 1)
    ids = jnp.concatenate([ids_ref[g : g + 1, :] for g in range(groups)], 1)
    hot_lhs = one_hot(lhs, 0, rows)
    h_re, h_im = pick(ent_re[...], hot_lhs, 3), pick(ent_im[...], hot_lhs, 3)
    for fetch in fetches[7:]:
        fetch.wait()
    chunk = 512

    def gather(c, carry):
        first = pl.multiple_of(c * chunk, chunk)
        hot = one_hot(ids, first, chunk)
        return (
            carry[0] + pick(rel_re[:, pl.ds(first, chunk)], hot, 3),
            carry[1] + pick(rel_im[:, pl.ds(first, chunk)], hot, 3),
        )

    empty = jnp.zeros((width, edges), F32)
    r_re, r_im = lax.fori_loop(0, rel_count // chunk, gather, (empty, empty))
    q_re = h_re * r_re - h_im * r_im
    q_im = h_re * r_im + h_im * r_re
    for g in range(groups):
        part = slice(g * per_edge, (g + 1) * per_edge)
        qs[g, 0:width, :] = q_re[:, part]
        qs[g, wp : wp + width, :] = q_im[:, part]

    for i in reversed(range(units)):
        for o in range(n_dim):
            td = other(o)
            s, g = unit(td, i)

            def near_query(g=g, i=i):
                qr[i, d] = qs[g]

            def far_query(s=s, g=g, i=i, o=o, td=td):
                remote(qs.at[g], qr.at[i, d], q_send.at[i, o], q_recv.at[i, d], (holder(-s), td)).start()

            if o == 0:
                when(s == 0, near_query)
                when(s != 0, far_query)
            else:
                far_query()

    for o in range(1, n_dim):
        wait_for(bf.at[other(o)], b_recv.at[other(o)])
    deep_k = n_dim * kp
    block = bf[...].reshape(deep_k, rows)
    for k, part in enumerate(split(block, 2)):
        bp[k] = part
    for k, part in enumerate(split(jnp.transpose(block), 3)):
        bt[k] = part

    at = lax.broadcasted_iota(jnp.int32, (rows, per_edge), 0)
    ones = jnp.ones((LANES, per_edge), BF16)

    def dot(a, b):
        return jnp.dot(a, b, preferred_element_type=F32)

    for i in range(units):
        s, g = unit(d, i)
        when(s != 0, lambda i=i: wait_for(mr.at[i], m_recv.at[i]))
        hits = jnp.zeros((rows, LANES), F32)
        for j in range(8):
            hits = hits + jnp.where(at == mr[i, j : j + 1, :], 1.0, 0.0)
        cnt = dot(hits.astype(BF16), ones)
        hit = at == mr[i, 8:9, :]
        live = jnp.where(mr[i, 9:10, :] == s, 1.0, 0.0)
        for o in range(n_dim):
            if o == 0:
                when(s != 0, lambda i=i: wait_for(qr.at[i, d], q_recv.at[i, d]))
            else:
                wait_for(qr.at[i, other(o)], q_recv.at[i, other(o)])
        q0, q1, q2 = split(qr[i].reshape(deep_k, per_edge), 3)
        b0, b1, b2 = bt[0], bt[1], bt[2]
        st = dot(b0, q0) + (dot(b0, q1) + dot(b1, q0)) + (dot(b0, q2) + dot(b2, q0) + dot(b1, q1))
        pos = jnp.sum(jnp.where(hit, st, 0.0), 0, keepdims=True)
        masked = jnp.where(cnt > 0.0, st, -3.0e38)
        top = jnp.maximum(jnp.max(masked, 0, keepdims=True), pos)
        e_neg = cnt * jnp.exp(masked - top)
        e_pos = jnp.exp(pos - top)
        scale = live / (e_pos + jnp.sum(e_neg, 0, keepdims=True))
        w = e_neg * scale + jnp.where(hit, e_pos * scale - live, 0.0)
        w0, w1 = split(w, 2)
        wts[0, :, i * per_edge : (i + 1) * per_edge] = w0
        wts[1, :, i * per_edge : (i + 1) * per_edge] = w1
        gq = dot(bp[0], w0) + (dot(bp[0], w1) + dot(bp[1], w0))
        gqo[i] = gq.reshape(n_dim, kp, per_edge)
        for o in range(n_dim):
            td = other(o)

            def near_grad(s=s, g=g, i=i):
                gqr[s, g] = gqo[i, d]

            def far_grad(s=s, g=g, i=i, o=o, td=td):
                remote(gqo.at[i, td], gqr.at[s, g], g_send.at[i, o], g_recv.at[s, g], (holder(s), td)).start()

            if o == 0:
                when(s == 0, near_grad)
                when(s != 0, far_grad)
            else:
                far_grad()
    q = jnp.concatenate([qr[i].reshape(deep_k, per_edge) for i in range(units)], 1)
    q0, q1 = split(q, 2)
    turned = (((1,), (1,)), ((), ()))
    gb = lax.dot_general(q0, wts[0], turned, preferred_element_type=F32)
    gb = gb + lax.dot_general(q0, wts[1], turned, preferred_element_type=F32)
    gb = gb + lax.dot_general(q1, wts[0], turned, preferred_element_type=F32)
    gbo[...] = gb.reshape(n_dim, kp, rows)
    for o in range(1, n_dim):
        remote(gbo.at[other(o)], gbr.at[d], e_send.at[o], e_recv.at[d], (p, other(o))).start()

    cols = []
    for g in range(groups):
        total = None
        for s in range(STEPS):
            handler = (s * groups + g) % n_dim
            if s == 0:
                when(d != handler, lambda s=s, g=g: wait_for(gqr.at[s, g], g_recv.at[s, g]))
            else:
                wait_for(gqr.at[s, g], g_recv.at[s, g])
            total = gqr[s, g] if total is None else total + gqr[s, g]
        cols.append(total)
    gq = jnp.concatenate(cols, 1)
    gq_re, gq_im = gq[0:width], gq[wp : wp + width]
    slots[p, 0, 0:width, :] = gq_re * h_re + gq_im * h_im
    slots[p, 1, 0:width, :] = gq_im * h_re - gq_re * h_im
    slots[p, 0, width : width + 1, :] = ids.astype(F32)

    def pass_on(j, half, way, target):
        remote(slots.at[j, half], slots.at[j, half], send.at[j, half, way], recv.at[j, half], (target, d)).start()

    def arrived(j, half):
        wait_for(slots.at[j, half], recv.at[j, half])

    def sent(j, half, way):
        wait_for(slots.at[j, half], send.at[j, half, way])

    def spread(j):
        pass_on(j, 0, 2, to_x)
        pass_on(j, 1, 3, to_y)
        pass_on(j, 0, 3, to_y)
        pass_on(j, 1, 2, to_x)

    def go_up(j):
        @pl.when(has_up)
        def _():
            pass_on(j, 0, 0, up)
            pass_on(j, 1, 0, up)

    def go_down(j):
        @pl.when(has_down)
        def _():
            pass_on(j, 0, 1, down)
            pass_on(j, 1, 1, down)

    go_up(p)
    go_down(p)
    spread(p)

    gent[...] = gbo[d]
    for o in range(1, n_dim):
        wait_for(gbr.at[other(o)], e_recv.at[other(o)])
        gent[...] += gbr[other(o)]
    gent[0:width, :] += put(gq_re * r_re + gq_im * r_im, hot_lhs, 2)
    gent[wp : wp + width, :] += put(gq_im * r_re - gq_re * r_im, hot_lhs, 2)
    g_re, g_im = gent[0:width, :], gent[wp : wp + width, :]
    esq[d] = jnp.sum(g_re * g_re, 0, keepdims=True) + jnp.sum(g_im * g_im, 0, keepdims=True)
    for o in range(1, n_dim):
        remote(esq.at[d], esq.at[d], eq_send.at[o], eq_recv.at[d], (p, other(o))).start()

    def cross(zz):
        from_x, from_y = index(zz, y, 1 - x), index(zz, 1 - y, x)
        arrived(from_x, 0)
        pass_on(from_x, 0, 3, to_y)
        arrived(from_y, 1)
        pass_on(from_y, 1, 2, to_x)

    def column(k, carry):
        below, above = z - k, z + k

        @pl.when(below >= 0)
        def _():
            j = index(below, y, x)
            arrived(j, 0)
            arrived(j, 1)
            go_up(j)
            spread(j)

        @pl.when(above < deep)
        def _():
            j = index(above, y, x)
            arrived(j, 0)
            arrived(j, 1)
            go_down(j)
            spread(j)

        @pl.when(below + 1 >= 0)
        def _():
            cross(below + 1)

        @pl.when((above - 1 < deep) & (k > 1))
        def _():
            cross(above - 1)

        return carry

    lax.fori_loop(1, deep, column, 0)
    for far in (z - (deep - 1), z + (deep - 1)):

        @pl.when((far >= 0) & (far < deep))
        def _(far=far):
            cross(far)

    per_batch = batch.shape[1] // edges
    piece = min(256, rel_count)
    labels = lax.broadcasted_iota(jnp.int32, (piece, per_batch * edges), 0).astype(F32).astype(BF16)

    def add_up(js, fresh):
        names = []
        for k, j in enumerate(js):
            cut = slice(k * edges, (k + 1) * edges)
            high, low = split(slots[j].reshape(kp, edges), 2)
            batch[0:kp, cut] = high
            batch[kp : 2 * kp, cut] = low
            names.append(slots[j, 0, width : width + 1, :])
        names = jnp.concatenate(names, 1)

        def body(c, carry):
            first = pl.multiple_of(c * piece, piece)
            mine = (names - first.astype(F32)).astype(BF16)
            hot = jnp.where(labels == mine, jnp.ones((), BF16), jnp.zeros((), BF16))
            both = lax.dot_general(batch[...], hot, turned, preferred_element_type=F32)
            total = both[0:kp] + both[kp : 2 * kp]
            if not fresh:
                total = total + acc[:, pl.ds(first, piece)]
            acc[:, pl.ds(first, piece)] = total
            return carry

        lax.fori_loop(0, rel_count // piece, body, 0)

    add_up([index(zz, y, x) for zz in range(per_batch)], True)
    for lot in range(1, deep // per_batch):
        add_up([index(lot * per_batch + zz, y, x) for zz in range(per_batch)], False)

    total = esq[d]
    for o in range(1, n_dim):
        wait_for(esq.at[other(o)], eq_recv.at[other(o)])
        total = total + esq[other(o)]
    total = ent_acc[...] + total / D
    new_acc[...] = total
    scale = RATE / jnp.sqrt(total)
    new_re[...] = ent_re[...] - scale * gent[0:width, :]
    new_im[...] = ent_im[...] - scale * gent[wp : wp + width, :]

    for yy, xx, halves in ((y, 1 - x, (1,)), (1 - y, x, (0,)), (1 - y, 1 - x, (0, 1))):

        def rest(lot, carry, yy=yy, xx=xx, halves=halves):
            js = [index(lot * per_batch + zz, yy, xx) for zz in range(per_batch)]
            for j in js:
                for half in halves:
                    arrived(j, half)
            add_up(js, False)
            return carry

        lax.fori_loop(0, deep // per_batch, rest, 0)

    t_re, t_im = acc[0:width, :], acc[wp : wp + width, :]
    rsq[d] = jnp.sum(t_re * t_re, 0, keepdims=True) + jnp.sum(t_im * t_im, 0, keepdims=True)
    for o in range(1, n_dim):
        remote(rsq.at[d], rsq.at[d], rq_send.at[o], rq_recv.at[d], (p, other(o))).start()
    total = rsq[d]
    for o in range(1, n_dim):
        wait_for(rsq.at[other(o)], rq_recv.at[other(o)])
        total = total + rsq[other(o)]
    total = rel_acc[...] + total / D
    new_racc[...] = total
    scale = RATE / jnp.sqrt(total)
    new_rre[...] = rel_re[...] - scale * acc[0:width, :]
    new_rim[...] = rel_im[...] - scale * acc[wp : wp + width, :]

    def drain(zz, carry):
        j = index(zz, y, x)
        for half in (0, 1):

            @pl.when((zz <= z) & has_up)
            def _(half=half):
                sent(j, half, 0)

            @pl.when((zz >= z) & has_down)
            def _(half=half):
                sent(j, half, 1)

            sent(j, half, 2)
            sent(j, half, 3)
        sent(index(zz, y, 1 - x), 0, 3)
        sent(index(zz, 1 - y, x), 1, 2)
        return carry

    lax.fori_loop(0, deep, drain, 0)
    for o in range(1, n_dim):
        wait_for(bf.at[d], b_send.at[o])
        wait_for(gbo.at[d], e_send.at[o])
        wait_for(esq.at[d], eq_send.at[o])
        wait_for(rsq.at[d], rq_send.at[o])
    for i in range(units):
        s, g = unit(d, i)
        when(s != 0, lambda i=i: wait_for(mt.at[0], m_send.at[i]))
        when(s != 0, lambda i=i: wait_for(qs.at[0], q_send.at[i, 0]))
        when(s != 0, lambda i=i: wait_for(gqo.at[i, 0], g_send.at[i, 0]))
        for o in range(1, n_dim):
            wait_for(qs.at[0], q_send.at[i, o])
            wait_for(gqo.at[i, 0], g_send.at[i, o])


def per_device(
    n_dom, n_dim,
    ent_re, ent_im, ent_acc, rel_re, rel_im, rel_acc, lhs_rows, rhs_rows, rel_ids, neg_rows, bucket_step,
):
    width, rows = ent_re.shape
    rel_count = rel_re.shape[1]
    groups, per_edge = lhs_rows.shape
    wp = (width // 8 + 1) * 8
    kp = 2 * wp
    units = groups * STEPS // n_dim
    edges = groups * per_edge
    deep_k = n_dim * kp
    vmem = pl.BlockSpec(memory_space=pltpu.VMEM)
    hbm = pl.BlockSpec(memory_space=pl.ANY)
    dma = pltpu.SemaphoreType.DMA
    shape = jax.ShapeDtypeStruct
    args = (
        ent_re, ent_im, ent_acc.reshape(1, rows), rel_re, rel_im, rel_acc.reshape(1, rel_count),
        lhs_rows, rhs_rows, rel_ids, neg_rows, bucket_step.reshape(1, groups),
    )
    outs = pl.pallas_call(
        functools.partial(round_kernel, n_dom, n_dim),
        out_shape=tuple(shape(a.shape, F32) for a in args[:6]),
        in_specs=[hbm] * len(args),
        out_specs=(vmem,) * 6,
        scratch_shapes=[pltpu.VMEM(a.shape, a.dtype) for a in args] + [
            pltpu.VMEM((groups, kp, per_edge), F32),
            pltpu.VMEM((units, n_dim, kp, per_edge), F32),
            pltpu.VMEM((groups, META, LANES), jnp.int32),
            pltpu.VMEM((units, META, LANES), jnp.int32),
            pltpu.VMEM((n_dim, kp, rows), F32),
            pltpu.VMEM((3, rows, deep_k), BF16),
            pltpu.VMEM((2, deep_k, rows), BF16),
            pltpu.VMEM((2, rows, units * per_edge), BF16),
            pltpu.VMEM((units, n_dim, kp, per_edge), F32),
            pltpu.VMEM((STEPS, groups, kp, per_edge), F32),
            pltpu.VMEM((n_dim, kp, rows), F32),
            pltpu.VMEM((n_dim, kp, rows), F32),
            pltpu.VMEM((kp, rows), F32),
            pltpu.VMEM((n_dom, 2, wp, edges), F32),
            pltpu.VMEM((kp, rel_count), F32),
            pltpu.VMEM((2 * kp, 4 * edges), BF16),
            pltpu.VMEM((n_dim, 1, rows), F32),
            pltpu.VMEM((n_dim, 1, rel_count), F32),
            dma((len(args),)),
            dma((units, n_dim)), dma((units, n_dim)),
            dma((units,)), dma((units,)),
            dma((n_dim,)), dma((n_dim,)),
            dma((units, n_dim)), dma((STEPS, groups)),
            dma((n_dim,)), dma((n_dim,)),
            dma((n_dom, 2, 4)), dma((n_dom, 2)),
            dma((n_dim,)), dma((n_dim,)),
            dma((n_dim,)), dma((n_dim,)),
        ],
        compiler_params=pltpu.CompilerParams(
            collective_id=0, has_side_effects=True, vmem_limit_bytes=60 * 1024 * 1024
        ),
    )(*args)
    return outs[0], outs[1], outs[2].reshape(rows), outs[3], outs[4], outs[5].reshape(rel_count)


def solution(mesh):
    return jax.shard_map(
        functools.partial(per_device, mesh.shape["dom"], mesh.shape["dim"]),
        mesh=mesh,
        in_specs=(
            P("dim", "dom"),
            P("dim", "dom"),
            P("dom"),
            P("dim", None),
            P("dim", None),
            P(),
            P("dom", None),
            P("dom", None),
            P("dom", None),
            P("dom", None),
            P("dom"),
        ),
        out_specs=(P("dim", "dom"), P("dim", "dom"), P("dom"), P("dim", None), P("dim", None), P()),
        check_vma=False,
    )
```

```python
import functools
import jax
import jax.numpy as jnp
from jax import lax
from jax.experimental import pallas as pl
from jax.experimental.pallas import tpu as pltpu
from jax.sharding import PartitionSpec as P

D = 400
STEPS = 4
RATE = 0.1
MESH = pl.DeviceIdType.MESH
F32 = jnp.float32
BF16 = jnp.bfloat16
META = 16
LANES = 128
PIECE = 256


def low_high(ids):
    high = lax.div(ids, PIECE)
    return ids - high * PIECE, high


def split(x, n):
    parts = []
    for _ in range(n):
        part = x.astype(BF16)
        parts.append(part)
        x = x - part.astype(F32)
    return parts


def one_hot(row, first, count):
    rows = lax.broadcasted_iota(jnp.int32, (count, row.shape[1]), 0) + first
    return jnp.where(rows == row, 1.0, 0.0).astype(BF16)


def pick(x, hot, n):
    total = None
    for part in split(x, n):
        term = jnp.dot(part, hot, preferred_element_type=F32)
        total = term if total is None else total + term
    return total


def put(x, hot, n):
    total = None
    for part in split(x, n):
        term = lax.dot_general(part, hot, (((1,), (1,)), ((), ())), preferred_element_type=F32)
        total = term if total is None else total + term
    return total


def when(pred, fn):
    if isinstance(pred, bool):
        if pred:
            fn()
    else:
        pl.when(pred)(fn)


def wait_for(ref, sem):
    pltpu.make_async_copy(ref, ref, sem).wait()


def remote(src, dst, send, recv, device):
    return pltpu.make_async_remote_copy(
        src_ref=src, dst_ref=dst, send_sem=send, recv_sem=recv, device_id=device, device_id_type=MESH
    )


def round_kernel(
    n_dom, n_dim,
    ent_re_in, ent_im_in, rel_re_in, rel_im_in, lhs_in, rhs_in, ids_in, neg_in, bs_in,
    gent_out, ent_sq, acc_out, rel_sq,
    ent_re, ent_im, rel_re, rel_im, lhs_ref, rhs_ref, ids_ref, neg_ref, bs_ref,
    qs, qr, mt, mr, bf, bt, bp, wts, gqo, gqr, gbo, gbr, gent,
    slots, acc, batch, hot_ref, esq, rsq,
    in_sem, out_sem,
    q_send, q_recv, m_send, m_recv, b_send, b_recv, g_send, g_recv, e_send, e_recv,
    send, recv, eq_send, eq_recv, rq_send, rq_recv,
):
    p, d = lax.axis_index("dom"), lax.axis_index("dim")
    width, rows = ent_re.shape
    groups, per_edge = lhs_ref.shape
    edges = groups * per_edge
    rel_count = rel_re.shape[1]
    kp = qs.shape[1]
    wp = kp // 2
    units = groups * STEPS // n_dim
    deep = n_dom // 4
    z, y, x = lax.div(p, 4), lax.rem(lax.div(p, 2), 2), lax.rem(p, 2)

    def index(zz, yy, xx):
        return zz * 4 + yy * 2 + xx

    def unit(td, i):
        if n_dim == groups:
            return i, td
        number = td + n_dim * i
        return lax.div(number, groups), lax.rem(number, groups)

    def holder(offset):
        return lax.rem(p + offset + n_dom, n_dom)

    def other(o):
        return lax.rem(d + o, n_dim)

    to_x, to_y = index(z, y, 1 - x), index(z, 1 - y, x)
    up, down = p + 4, p - 4
    has_up, has_down = z < deep - 1, z > 0

    barrier = pltpu.get_barrier_semaphore()

    def greet(dom, dim):
        pl.semaphore_signal(barrier, inc=1, device_id=(dom, dim), device_id_type=MESH)

    peers = 0
    for offset in range(1 - STEPS, STEPS):
        for o in range(n_dim):
            if offset != 0 or o != 0:
                greet(holder(offset), other(o))
                peers += 1
    greet(to_x, d)
    greet(to_y, d)

    @pl.when(has_up)
    def _():
        greet(up, d)

    @pl.when(has_down)
    def _():
        greet(down, d)

    fetches = []
    for k, (src, dst) in enumerate([
        (lhs_in, lhs_ref), (rhs_in, rhs_ref), (ids_in, ids_ref), (neg_in, neg_ref), (bs_in, bs_ref),
        (ent_re_in, ent_re), (ent_im_in, ent_im), (rel_re_in, rel_re), (rel_im_in, rel_im),
    ]):
        fetches.append(pltpu.make_async_copy(src, dst, in_sem.at[k]))
        fetches[-1].start()
    mt[...] = jnp.full(mt.shape, -1, jnp.int32)
    qs[...] = jnp.zeros(qs.shape, F32)
    for half in (0, 1):
        slots[p, half] = jnp.zeros((wp, edges), F32)
    bf[d] = jnp.zeros((kp, rows), F32)
    for fetch in fetches[:7]:
        fetch.wait()

    n_neg = neg_ref.shape[1]
    for g in range(groups):
        for j in range(0, n_neg, LANES):
            wide = min(LANES, n_neg - j)
            mt[g, j // LANES : j // LANES + 1, 0:wide] = neg_ref[g : g + 1, j : j + wide]
        mt[g, 8:9, :] = rhs_ref[g : g + 1, :]
        mt[g, 9:10, :] = jnp.broadcast_to(bs_ref[:, g : g + 1], (1, LANES))
    bf[d, 0:width, :] = ent_re[...]
    bf[d, wp : wp + width, :] = ent_im[...]

    pl.semaphore_wait(barrier, peers + 2 + jnp.minimum(z, 1) + jnp.minimum(deep - 1 - z, 1))

    for i in range(units):
        s, g = unit(d, i)

        def local_meta(g=g, i=i):
            mr[i] = mt[g]

        def far_meta(s=s, g=g, i=i):
            remote(mt.at[g], mr.at[i], m_send.at[i], m_recv.at[i], (holder(-s), d)).start()

        when(s == 0, local_meta)
        when(s != 0, far_meta)
    for o in range(1, n_dim):
        remote(bf.at[d], bf.at[d], b_send.at[o], b_recv.at[d], (p, other(o))).start()

    lhs = jnp.concatenate([lhs_ref[g : g + 1, :] for g in range(groups)], 1)
    ids = jnp.concatenate([ids_ref[g : g + 1, :] for g in range(groups)], 1)
    hot_lhs = one_hot(lhs, 0, rows)
    h_re, h_im = pick(ent_re[...], hot_lhs, 3), pick(ent_im[...], hot_lhs, 3)
    for fetch in fetches[7:]:
        fetch.wait()
    base, high_of = low_high(ids)
    hot_ids = one_hot(base, 0, PIECE)

    def gather(c, carry):
        first = pl.multiple_of(c * PIECE, PIECE)
        here = high_of == c
        return (
            jnp.where(here, pick(rel_re[:, pl.ds(first, PIECE)], hot_ids, 3), carry[0]),
            jnp.where(here, pick(rel_im[:, pl.ds(first, PIECE)], hot_ids, 3), carry[1]),
        )

    empty = jnp.zeros((width, edges), F32)
    r_re, r_im = lax.fori_loop(0, rel_count // PIECE, gather, (empty, empty))
    q_re = h_re * r_re - h_im * r_im
    q_im = h_re * r_im + h_im * r_re
    for g in range(groups):
        part = slice(g * per_edge, (g + 1) * per_edge)
        qs[g, 0:width, :] = q_re[:, part]
        qs[g, wp : wp + width, :] = q_im[:, part]

    for i in reversed(range(units)):
        for o in range(n_dim):
            td = other(o)
            s, g = unit(td, i)

            def near_query(g=g, i=i):
                qr[i, d] = qs[g]

            def far_query(s=s, g=g, i=i, o=o, td=td):
                remote(qs.at[g], qr.at[i, d], q_send.at[i, o], q_recv.at[i, d], (holder(-s), td)).start()

            if o == 0:
                when(s == 0, near_query)
                when(s != 0, far_query)
            else:
                far_query()

    for o in range(1, n_dim):
        wait_for(bf.at[other(o)], b_recv.at[other(o)])
    deep_k = n_dim * kp
    block = bf[...].reshape(deep_k, rows)
    for k, part in enumerate(split(block, 2)):
        bp[k] = part
    for k, part in enumerate(split(jnp.transpose(block), 3)):
        bt[k] = part

    at = lax.broadcasted_iota(jnp.int32, (rows, per_edge), 0)
    ones = jnp.ones((LANES, per_edge), BF16)

    def dot(a, b):
        return jnp.dot(a, b, preferred_element_type=F32)

    for i in range(units):
        s, g = unit(d, i)
        when(s != 0, lambda i=i: wait_for(mr.at[i], m_recv.at[i]))
        hits = jnp.zeros((rows, LANES), F32)
        for j in range(8):
            hits = hits + jnp.where(at == mr[i, j : j + 1, :], 1.0, 0.0)
        cnt = dot(hits.astype(BF16), ones)
        hit = at == mr[i, 8:9, :]
        live = jnp.where(mr[i, 9:10, :] == s, 1.0, 0.0)
        for o in range(n_dim):
            if o == 0:
                when(s != 0, lambda i=i: wait_for(qr.at[i, d], q_recv.at[i, d]))
            else:
                wait_for(qr.at[i, other(o)], q_recv.at[i, other(o)])
        q0, q1, q2 = split(qr[i].reshape(deep_k, per_edge), 3)
        b0, b1, b2 = bt[0], bt[1], bt[2]
        st = dot(b0, q0) + (dot(b0, q1) + dot(b1, q0)) + (dot(b0, q2) + dot(b2, q0) + dot(b1, q1))
        pos = jnp.sum(jnp.where(hit, st, 0.0), 0, keepdims=True)
        masked = jnp.where(cnt > 0.0, st, -3.0e38)
        top = jnp.maximum(jnp.max(masked, 0, keepdims=True), pos)
        e_neg = cnt * jnp.exp(masked - top)
        e_pos = jnp.exp(pos - top)
        scale = live / (e_pos + jnp.sum(e_neg, 0, keepdims=True))
        w = e_neg * scale + jnp.where(hit, e_pos * scale - live, 0.0)
        w0, w1 = split(w, 2)
        wts[0, :, i * per_edge : (i + 1) * per_edge] = w0
        wts[1, :, i * per_edge : (i + 1) * per_edge] = w1
        gq = dot(bp[0], w0) + (dot(bp[0], w1) + dot(bp[1], w0))
        gqo[i] = gq.reshape(n_dim, kp, per_edge)
        for o in range(n_dim):
            td = other(o)

            def near_grad(s=s, g=g, i=i):
                gqr[s, g] = gqo[i, d]

            def far_grad(s=s, g=g, i=i, o=o, td=td):
                remote(gqo.at[i, td], gqr.at[s, g], g_send.at[i, o], g_recv.at[s, g], (holder(s), td)).start()

            if o == 0:
                when(s == 0, near_grad)
                when(s != 0, far_grad)
            else:
                far_grad()
    q = jnp.concatenate([qr[i].reshape(deep_k, per_edge) for i in range(units)], 1)
    q0, q1 = split(q, 2)
    turned = (((1,), (1,)), ((), ()))
    gb = lax.dot_general(q0, wts[0], turned, preferred_element_type=F32)
    gb = gb + lax.dot_general(q0, wts[1], turned, preferred_element_type=F32)
    gb = gb + lax.dot_general(q1, wts[0], turned, preferred_element_type=F32)
    gbo[...] = gb.reshape(n_dim, kp, rows)
    for o in range(1, n_dim):
        remote(gbo.at[other(o)], gbr.at[d], e_send.at[o], e_recv.at[d], (p, other(o))).start()

    cols = []
    for g in range(groups):
        total = None
        for s in range(STEPS):
            handler = (s * groups + g) % n_dim
            if s == 0:
                when(d != handler, lambda s=s, g=g: wait_for(gqr.at[s, g], g_recv.at[s, g]))
            else:
                wait_for(gqr.at[s, g], g_recv.at[s, g])
            total = gqr[s, g] if total is None else total + gqr[s, g]
        cols.append(total)
    gq = jnp.concatenate(cols, 1)
    gq_re, gq_im = gq[0:width], gq[wp : wp + width]
    slots[p, 0, 0:width, :] = gq_re * h_re + gq_im * h_im
    slots[p, 1, 0:width, :] = gq_im * h_re - gq_re * h_im
    slots[p, 0, width : width + 1, :] = ids.astype(F32)

    def pass_on(j, half, way, target):
        remote(slots.at[j, half], slots.at[j, half], send.at[j, half, way], recv.at[j, half], (target, d)).start()

    def arrived(j, half):
        wait_for(slots.at[j, half], recv.at[j, half])

    def sent(j, half, way):
        wait_for(slots.at[j, half], send.at[j, half, way])

    def spread(j):
        pass_on(j, 0, 2, to_x)
        pass_on(j, 1, 3, to_y)
        pass_on(j, 0, 3, to_y)
        pass_on(j, 1, 2, to_x)

    def go_up(j):
        @pl.when(has_up)
        def _():
            pass_on(j, 0, 0, up)
            pass_on(j, 1, 0, up)

    def go_down(j):
        @pl.when(has_down)
        def _():
            pass_on(j, 0, 1, down)
            pass_on(j, 1, 1, down)

    go_up(p)
    go_down(p)
    spread(p)

    gent[...] = gbo[d]
    for o in range(1, n_dim):
        wait_for(gbr.at[other(o)], e_recv.at[other(o)])
        gent[...] += gbr[other(o)]
    gent[0:width, :] += put(gq_re * r_re + gq_im * r_im, hot_lhs, 2)
    gent[wp : wp + width, :] += put(gq_im * r_re - gq_re * r_im, hot_lhs, 2)
    gent_copy = pltpu.make_async_copy(gent, gent_out, out_sem.at[0])
    gent_copy.start()
    g_re, g_im = gent[0:width, :], gent[wp : wp + width, :]
    esq[d] = jnp.sum(g_re * g_re, 0, keepdims=True) + jnp.sum(g_im * g_im, 0, keepdims=True)
    for o in range(1, n_dim):
        remote(esq.at[d], esq.at[d], eq_send.at[o], eq_recv.at[d], (p, other(o))).start()

    def cross(zz):
        from_x, from_y = index(zz, y, 1 - x), index(zz, 1 - y, x)
        arrived(from_x, 0)
        pass_on(from_x, 0, 3, to_y)
        arrived(from_y, 1)
        pass_on(from_y, 1, 2, to_x)

    def column(k, carry):
        below, above = z - k, z + k

        @pl.when(below >= 0)
        def _():
            j = index(below, y, x)
            arrived(j, 0)
            arrived(j, 1)
            go_up(j)
            spread(j)

        @pl.when(above < deep)
        def _():
            j = index(above, y, x)
            arrived(j, 0)
            arrived(j, 1)
            go_down(j)
            spread(j)

        @pl.when(below + 1 >= 0)
        def _():
            cross(below + 1)

        @pl.when((above - 1 < deep) & (k > 1))
        def _():
            cross(above - 1)

        return carry

    lax.fori_loop(1, deep, column, 0)
    for far in (z - (deep - 1), z + (deep - 1)):

        @pl.when((far >= 0) & (far < deep))
        def _(far=far):
            cross(far)

    per_batch = batch.shape[1] // edges
    lanes = lax.broadcasted_iota(jnp.int32, (edges, PIECE), 1)

    def add_up(js, fresh):
        highs = []
        for k, j in enumerate(js):
            cut = slice(k * edges, (k + 1) * edges)
            high, low = split(slots[j].reshape(kp, edges), 2)
            batch[0:kp, cut] = high
            batch[kp : 2 * kp, cut] = low
            base, piece_of = low_high(slots[j, 0, width : width + 1, :].astype(jnp.int32))
            down_rows = jnp.transpose(jnp.broadcast_to(base.astype(F32), (LANES, edges))).astype(jnp.int32)
            wide = jnp.concatenate([down_rows] * (PIECE // LANES), 1)
            hot_ref[cut, :] = jnp.where(lanes == wide, 1.0, 0.0).astype(BF16)
            highs.append(piece_of)
        highs = jnp.concatenate(highs, 1).astype(F32).astype(BF16)

        def body(c, carry):
            first = pl.multiple_of(c * PIECE, PIECE)
            here = highs == c.astype(F32).astype(BF16)
            mine = jnp.where(here, batch[...], jnp.zeros((), BF16))
            both = jnp.dot(mine, hot_ref[...], preferred_element_type=F32)
            total = both[0:kp] + both[kp : 2 * kp]
            if not fresh:
                total = total + acc[:, pl.ds(first, PIECE)]
            acc[:, pl.ds(first, PIECE)] = total
            return carry

        lax.fori_loop(0, rel_count // PIECE, body, 0)

    add_up([index(zz, y, x) for zz in range(per_batch)], True)
    for lot in range(1, deep // per_batch):
        add_up([index(lot * per_batch + zz, y, x) for zz in range(per_batch)], False)

    total = esq[d]
    for o in range(1, n_dim):
        wait_for(esq.at[other(o)], eq_recv.at[other(o)])
        total = total + esq[other(o)]
    ent_sq[...] = total

    for yy, xx, halves in ((y, 1 - x, (1,)), (1 - y, x, (0,)), (1 - y, 1 - x, (0, 1))):

        def rest(lot, carry, yy=yy, xx=xx, halves=halves):
            js = [index(lot * per_batch + zz, yy, xx) for zz in range(per_batch)]
            for j in js:
                for half in halves:
                    arrived(j, half)
            add_up(js, False)
            return carry

        lax.fori_loop(0, deep // per_batch, rest, 0)

    acc_copy = pltpu.make_async_copy(acc, acc_out, out_sem.at[1])
    acc_copy.start()
    t_re, t_im = acc[0:width, :], acc[wp : wp + width, :]
    rsq[d] = jnp.sum(t_re * t_re, 0, keepdims=True) + jnp.sum(t_im * t_im, 0, keepdims=True)
    for o in range(1, n_dim):
        remote(rsq.at[d], rsq.at[d], rq_send.at[o], rq_recv.at[d], (p, other(o))).start()
    total = rsq[d]
    for o in range(1, n_dim):
        wait_for(rsq.at[other(o)], rq_recv.at[other(o)])
        total = total + rsq[other(o)]
    rel_sq[...] = total

    def drain(zz, carry):
        j = index(zz, y, x)
        for half in (0, 1):

            @pl.when((zz <= z) & has_up)
            def _(half=half):
                sent(j, half, 0)

            @pl.when((zz >= z) & has_down)
            def _(half=half):
                sent(j, half, 1)

            sent(j, half, 2)
            sent(j, half, 3)
        sent(index(zz, y, 1 - x), 0, 3)
        sent(index(zz, 1 - y, x), 1, 2)
        return carry

    lax.fori_loop(0, deep, drain, 0)
    gent_copy.wait()
    acc_copy.wait()
    for o in range(1, n_dim):
        wait_for(bf.at[d], b_send.at[o])
        wait_for(gbo.at[d], e_send.at[o])
        wait_for(esq.at[d], eq_send.at[o])
        wait_for(rsq.at[d], rq_send.at[o])
    for i in range(units):
        s, g = unit(d, i)
        when(s != 0, lambda i=i: wait_for(mt.at[0], m_send.at[i]))
        when(s != 0, lambda i=i: wait_for(qs.at[0], q_send.at[i, 0]))
        when(s != 0, lambda i=i: wait_for(gqo.at[i, 0], g_send.at[i, 0]))
        for o in range(1, n_dim):
            wait_for(qs.at[0], q_send.at[i, o])
            wait_for(gqo.at[i, 0], g_send.at[i, o])


def update_kernel(
    gent, ent_sq, ent_re, ent_im, ent_acc, acc, rel_sq, rel_re, rel_im, rel_acc,
    new_re, new_im, new_acc, new_rre, new_rim, new_racc,
):
    width, wp = ent_re.shape[0], gent.shape[0] // 2
    for grad, sq, old_re, old_im, old, out_re, out_im, out in (
        (gent, ent_sq, ent_re, ent_im, ent_acc, new_re, new_im, new_acc),
        (acc, rel_sq, rel_re, rel_im, rel_acc, new_rre, new_rim, new_racc),
    ):
        total = old[...] + sq[...] / D
        out[...] = total
        scale = RATE / jnp.sqrt(total)
        out_re[...] = old_re[...] - scale * grad[0:width, :]
        out_im[...] = old_im[...] - scale * grad[wp : wp + width, :]


def per_device(
    n_dom, n_dim,
    ent_re, ent_im, ent_acc, rel_re, rel_im, rel_acc, lhs_rows, rhs_rows, rel_ids, neg_rows, bucket_step,
):
    width, rows = ent_re.shape
    rel_count = rel_re.shape[1]
    groups, per_edge = lhs_rows.shape
    wp = (width // 8 + 1) * 8
    kp = 2 * wp
    units = groups * STEPS // n_dim
    edges = groups * per_edge
    deep_k = n_dim * kp
    vmem = pl.BlockSpec(memory_space=pltpu.VMEM)
    hbm = pl.BlockSpec(memory_space=pl.ANY)
    dma = pltpu.SemaphoreType.DMA
    shape = jax.ShapeDtypeStruct
    args = (
        ent_re, ent_im, rel_re, rel_im,
        lhs_rows, rhs_rows, rel_ids, neg_rows, bucket_step.reshape(1, groups),
    )
    gent, ent_sq, acc, rel_sq = pl.pallas_call(
        functools.partial(round_kernel, n_dom, n_dim),
        out_shape=(
            shape((kp, rows), F32), shape((1, rows), F32), shape((kp, rel_count), F32), shape((1, rel_count), F32)
        ),
        in_specs=[hbm] * len(args),
        out_specs=(hbm, vmem, hbm, vmem),
        scratch_shapes=[pltpu.VMEM(a.shape, a.dtype) for a in args] + [
            pltpu.VMEM((groups, kp, per_edge), F32),
            pltpu.VMEM((units, n_dim, kp, per_edge), F32),
            pltpu.VMEM((groups, META, LANES), jnp.int32),
            pltpu.VMEM((units, META, LANES), jnp.int32),
            pltpu.VMEM((n_dim, kp, rows), F32),
            pltpu.VMEM((3, rows, deep_k), BF16),
            pltpu.VMEM((2, deep_k, rows), BF16),
            pltpu.VMEM((2, rows, units * per_edge), BF16),
            pltpu.VMEM((units, n_dim, kp, per_edge), F32),
            pltpu.VMEM((STEPS, groups, kp, per_edge), F32),
            pltpu.VMEM((n_dim, kp, rows), F32),
            pltpu.VMEM((n_dim, kp, rows), F32),
            pltpu.VMEM((kp, rows), F32),
            pltpu.VMEM((n_dom, 2, wp, edges), F32),
            pltpu.VMEM((kp, rel_count), F32),
            pltpu.VMEM((2 * kp, 4 * edges), BF16),
            pltpu.VMEM((4 * edges, PIECE), BF16),
            pltpu.VMEM((n_dim, 1, rows), F32),
            pltpu.VMEM((n_dim, 1, rel_count), F32),
            dma((len(args),)), dma((2,)),
            dma((units, n_dim)), dma((units, n_dim)),
            dma((units,)), dma((units,)),
            dma((n_dim,)), dma((n_dim,)),
            dma((units, n_dim)), dma((STEPS, groups)),
            dma((n_dim,)), dma((n_dim,)),
            dma((n_dom, 2, 4)), dma((n_dom, 2)),
            dma((n_dim,)), dma((n_dim,)),
            dma((n_dim,)), dma((n_dim,)),
        ],
        compiler_params=pltpu.CompilerParams(
            collective_id=0, has_side_effects=True, vmem_limit_bytes=60 * 1024 * 1024
        ),
    )(*args)
    steps = rows // LANES
    ent, ent_row = pl.BlockSpec((width, LANES), lambda c: (0, c)), pl.BlockSpec((1, LANES), lambda c: (0, c))
    some = rel_count // steps
    rel, rel_row = pl.BlockSpec((width, some), lambda c: (0, c)), pl.BlockSpec((1, some), lambda c: (0, c))
    outs = pl.pallas_call(
        update_kernel,
        grid=(steps,),
        out_shape=tuple(shape(s, F32) for s in (
            (width, rows), (width, rows), (1, rows), (width, rel_count), (width, rel_count), (1, rel_count)
        )),
        in_specs=[
            pl.BlockSpec((kp, LANES), lambda c: (0, c)), ent_row, ent, ent, ent_row,
            pl.BlockSpec((kp, some), lambda c: (0, c)), rel_row, rel, rel, rel_row,
        ],
        out_specs=(ent, ent, ent_row, rel, rel, rel_row),
        compiler_params=pltpu.CompilerParams(vmem_limit_bytes=60 * 1024 * 1024),
    )(
        gent, ent_sq, ent_re, ent_im, ent_acc.reshape(1, rows),
        acc, rel_sq, rel_re, rel_im, rel_acc.reshape(1, rel_count),
    )
    return outs[0], outs[1], outs[2].reshape(rows), outs[3], outs[4], outs[5].reshape(rel_count)


def solution(mesh):
    return jax.shard_map(
        functools.partial(per_device, mesh.shape["dom"], mesh.shape["dim"]),
        mesh=mesh,
        in_specs=(
            P("dim", "dom"),
            P("dim", "dom"),
            P("dom"),
            P("dim", None),
            P("dim", None),
            P(),
            P("dom", None),
            P("dom", None),
            P("dom", None),
            P("dom", None),
            P("dom"),
        ),
        out_specs=(P("dim", "dom"), P("dim", "dom"), P("dom"), P("dim", None), P("dim", None), P()),
        check_vma=False,
    )
```

```python
import functools
import jax
import jax.numpy as jnp
from jax import lax
from jax.experimental import pallas as pl
from jax.experimental.pallas import tpu as pltpu
from jax.sharding import PartitionSpec as P

D = 400
STEPS = 4
RATE = 0.1
MESH = pl.DeviceIdType.MESH
F32 = jnp.float32
BF16 = jnp.bfloat16
META = 16
LANES = 128
PIECE = 256


def low_high(ids):
    high = lax.div(ids, PIECE)
    return ids - high * PIECE, high


def split(x, n):
    parts = []
    for _ in range(n):
        part = x.astype(BF16)
        parts.append(part)
        x = x - part.astype(F32)
    return parts


def one_hot(row, first, count):
    rows = lax.broadcasted_iota(jnp.int32, (count, row.shape[1]), 0) + first
    return jnp.where(rows == row, 1.0, 0.0).astype(BF16)


def pick(x, hot, n):
    total = None
    for part in split(x, n):
        term = jnp.dot(part, hot, preferred_element_type=F32)
        total = term if total is None else total + term
    return total


def put(x, hot, n):
    total = None
    for part in split(x, n):
        term = lax.dot_general(part, hot, (((1,), (1,)), ((), ())), preferred_element_type=F32)
        total = term if total is None else total + term
    return total


def when(pred, fn):
    if isinstance(pred, bool):
        if pred:
            fn()
    else:
        pl.when(pred)(fn)


def wait_for(ref, sem):
    pltpu.make_async_copy(ref, ref, sem).wait()


def remote(src, dst, send, recv, device):
    return pltpu.make_async_remote_copy(
        src_ref=src, dst_ref=dst, send_sem=send, recv_sem=recv, device_id=device, device_id_type=MESH
    )


def round_kernel(
    n_dom, n_dim,
    ent_re_in, ent_im_in, rel_re_in, rel_im_in, lhs_in, rhs_in, ids_in, neg_in, bs_in,
    gent_out, ent_sq, acc_out, rel_sq,
    ent_re, ent_im, rel_re, rel_im, lhs_ref, rhs_ref, ids_ref, neg_ref, bs_ref,
    qs, qr, mt, mr, bf, bt, bp, wts, gqo, gqr, gbo, gbr, gent,
    slots, acc, batch, hot_ref, esq, rsq,
    in_sem, out_sem,
    q_send, q_recv, m_send, m_recv, b_send, b_recv, g_send, g_recv, e_send, e_recv,
    send, recv, eq_send, eq_recv, rq_send, rq_recv,
):
    p, d = lax.axis_index("dom"), lax.axis_index("dim")
    width, rows = ent_re.shape
    groups, per_edge = lhs_ref.shape
    edges = groups * per_edge
    rel_count = rel_re.shape[1]
    kp = qs.shape[1]
    wp = kp // 2
    units = groups * STEPS // n_dim
    deep = n_dom // 4
    z, y, x = lax.div(p, 4), lax.rem(lax.div(p, 2), 2), lax.rem(p, 2)

    def index(zz, yy, xx):
        return zz * 4 + yy * 2 + xx

    def unit(td, i):
        if n_dim == groups:
            return i, td
        number = td + n_dim * i
        return lax.div(number, groups), lax.rem(number, groups)

    def holder(offset):
        return lax.rem(p + offset + n_dom, n_dom)

    def other(o):
        return lax.rem(d + o, n_dim)

    to_x, to_y = index(z, y, 1 - x), index(z, 1 - y, x)
    up, down = p + 4, p - 4
    has_up, has_down = z < deep - 1, z > 0

    barrier = pltpu.get_barrier_semaphore()

    def greet(dom, dim):
        pl.semaphore_signal(barrier, inc=1, device_id=(dom, dim), device_id_type=MESH)

    peers = 0
    for offset in range(1 - STEPS, STEPS):
        for o in range(n_dim):
            if offset != 0 or o != 0:
                greet(holder(offset), other(o))
                peers += 1
    greet(to_x, d)
    greet(to_y, d)

    @pl.when(has_up)
    def _():
        greet(up, d)

    @pl.when(has_down)
    def _():
        greet(down, d)

    fetches = []
    for k, (src, dst) in enumerate([
        (lhs_in, lhs_ref), (rhs_in, rhs_ref), (ids_in, ids_ref), (neg_in, neg_ref), (bs_in, bs_ref),
        (ent_re_in, ent_re), (ent_im_in, ent_im), (rel_re_in, rel_re), (rel_im_in, rel_im),
    ]):
        fetches.append(pltpu.make_async_copy(src, dst, in_sem.at[k]))
        fetches[-1].start()
    mt[...] = jnp.full(mt.shape, -1, jnp.int32)
    qs[...] = jnp.zeros(qs.shape, F32)
    slots[p] = jnp.zeros((kp, edges), F32)
    bf[d] = jnp.zeros((kp, rows), F32)
    for fetch in fetches[:7]:
        fetch.wait()

    n_neg = neg_ref.shape[1]
    for g in range(groups):
        for j in range(0, n_neg, LANES):
            wide = min(LANES, n_neg - j)
            mt[g, j // LANES : j // LANES + 1, 0:wide] = neg_ref[g : g + 1, j : j + wide]
        mt[g, 8:9, :] = rhs_ref[g : g + 1, :]
        mt[g, 9:10, :] = jnp.broadcast_to(bs_ref[:, g : g + 1], (1, LANES))
    bf[d, 0:width, :] = ent_re[...]
    bf[d, wp : wp + width, :] = ent_im[...]

    pl.semaphore_wait(barrier, peers + 2 + jnp.minimum(z, 1) + jnp.minimum(deep - 1 - z, 1))

    for i in range(units):
        s, g = unit(d, i)

        def local_meta(g=g, i=i):
            mr[i] = mt[g]

        def far_meta(s=s, g=g, i=i):
            remote(mt.at[g], mr.at[i], m_send.at[i], m_recv.at[i], (holder(-s), d)).start()

        when(s == 0, local_meta)
        when(s != 0, far_meta)
    for o in range(1, n_dim):
        remote(bf.at[d], bf.at[d], b_send.at[o], b_recv.at[d], (p, other(o))).start()

    lhs = jnp.concatenate([lhs_ref[g : g + 1, :] for g in range(groups)], 1)
    ids = jnp.concatenate([ids_ref[g : g + 1, :] for g in range(groups)], 1)
    hot_lhs = one_hot(lhs, 0, rows)
    h_re, h_im = pick(ent_re[...], hot_lhs, 3), pick(ent_im[...], hot_lhs, 3)
    for fetch in fetches[7:]:
        fetch.wait()
    base, high_of = low_high(ids)
    hot_ids = one_hot(base, 0, PIECE)

    def gather(c, carry):
        first = pl.multiple_of(c * PIECE, PIECE)
        here = high_of == c
        return (
            jnp.where(here, pick(rel_re[:, pl.ds(first, PIECE)], hot_ids, 3), carry[0]),
            jnp.where(here, pick(rel_im[:, pl.ds(first, PIECE)], hot_ids, 3), carry[1]),
        )

    empty = jnp.zeros((width, edges), F32)
    r_re, r_im = lax.fori_loop(0, rel_count // PIECE, gather, (empty, empty))
    q_re = h_re * r_re - h_im * r_im
    q_im = h_re * r_im + h_im * r_re
    for g in range(groups):
        part = slice(g * per_edge, (g + 1) * per_edge)
        qs[g, 0:width, :] = q_re[:, part]
        qs[g, wp : wp + width, :] = q_im[:, part]

    for i in reversed(range(units)):
        for o in range(n_dim):
            td = other(o)
            s, g = unit(td, i)

            def near_query(g=g, i=i):
                qr[i, d] = qs[g]

            def far_query(s=s, g=g, i=i, o=o, td=td):
                remote(qs.at[g], qr.at[i, d], q_send.at[i, o], q_recv.at[i, d], (holder(-s), td)).start()

            if o == 0:
                when(s == 0, near_query)
                when(s != 0, far_query)
            else:
                far_query()

    for o in range(1, n_dim):
        wait_for(bf.at[other(o)], b_recv.at[other(o)])
    deep_k = n_dim * kp
    block = bf[...].reshape(deep_k, rows)
    for k, part in enumerate(split(block, 2)):
        bp[k] = part
    for k, part in enumerate(split(jnp.transpose(block), 3)):
        bt[k] = part

    at = lax.broadcasted_iota(jnp.int32, (rows, per_edge), 0)
    ones = jnp.ones((LANES, per_edge), BF16)

    def dot(a, b):
        return jnp.dot(a, b, preferred_element_type=F32)

    for i in range(units):
        s, g = unit(d, i)
        when(s != 0, lambda i=i: wait_for(mr.at[i], m_recv.at[i]))
        hits = jnp.zeros((rows, LANES), F32)
        for j in range(8):
            hits = hits + jnp.where(at == mr[i, j : j + 1, :], 1.0, 0.0)
        cnt = dot(hits.astype(BF16), ones)
        hit = at == mr[i, 8:9, :]
        live = jnp.where(mr[i, 9:10, :] == s, 1.0, 0.0)
        for o in range(n_dim):
            if o == 0:
                when(s != 0, lambda i=i: wait_for(qr.at[i, d], q_recv.at[i, d]))
            else:
                wait_for(qr.at[i, other(o)], q_recv.at[i, other(o)])
        q0, q1, q2 = split(qr[i].reshape(deep_k, per_edge), 3)
        b0, b1, b2 = bt[0], bt[1], bt[2]
        st = dot(b0, q0) + (dot(b0, q1) + dot(b1, q0)) + (dot(b0, q2) + dot(b2, q0) + dot(b1, q1))
        pos = jnp.sum(jnp.where(hit, st, 0.0), 0, keepdims=True)
        masked = jnp.where(cnt > 0.0, st, -3.0e38)
        top = jnp.maximum(jnp.max(masked, 0, keepdims=True), pos)
        e_neg = cnt * jnp.exp(masked - top)
        e_pos = jnp.exp(pos - top)
        scale = live / (e_pos + jnp.sum(e_neg, 0, keepdims=True))
        w = e_neg * scale + jnp.where(hit, e_pos * scale - live, 0.0)
        w0, w1 = split(w, 2)
        wts[0, :, i * per_edge : (i + 1) * per_edge] = w0
        wts[1, :, i * per_edge : (i + 1) * per_edge] = w1
        gq = dot(bp[0], w0) + (dot(bp[0], w1) + dot(bp[1], w0))
        gqo[i] = gq.reshape(n_dim, kp, per_edge)
        for o in range(n_dim):
            td = other(o)

            def near_grad(s=s, g=g, i=i):
                gqr[s, g] = gqo[i, d]

            def far_grad(s=s, g=g, i=i, o=o, td=td):
                remote(gqo.at[i, td], gqr.at[s, g], g_send.at[i, o], g_recv.at[s, g], (holder(s), td)).start()

            if o == 0:
                when(s == 0, near_grad)
                when(s != 0, far_grad)
            else:
                far_grad()
    q = jnp.concatenate([qr[i].reshape(deep_k, per_edge) for i in range(units)], 1)
    q0, q1 = split(q, 2)
    turned = (((1,), (1,)), ((), ()))
    gb = lax.dot_general(q0, wts[0], turned, preferred_element_type=F32)
    gb = gb + lax.dot_general(q0, wts[1], turned, preferred_element_type=F32)
    gb = gb + lax.dot_general(q1, wts[0], turned, preferred_element_type=F32)
    gbo[...] = gb.reshape(n_dim, kp, rows)
    for o in range(1, n_dim):
        remote(gbo.at[other(o)], gbr.at[d], e_send.at[o], e_recv.at[d], (p, other(o))).start()

    cols = []
    for g in range(groups):
        total = None
        for s in range(STEPS):
            handler = (s * groups + g) % n_dim
            if s == 0:
                when(d != handler, lambda s=s, g=g: wait_for(gqr.at[s, g], g_recv.at[s, g]))
            else:
                wait_for(gqr.at[s, g], g_recv.at[s, g])
            total = gqr[s, g] if total is None else total + gqr[s, g]
        cols.append(total)
    gq = jnp.concatenate(cols, 1)
    gq_re, gq_im = gq[0:width], gq[wp : wp + width]
    slots[p, 0:width, :] = gq_re * h_re + gq_im * h_im
    slots[p, wp : wp + width, :] = gq_im * h_re - gq_re * h_im
    slots[p, width : width + 1, :] = ids.astype(F32)

    thin = max(1, (kp // 8 + 4) // 9) * 8
    thick = (kp - 2 * thin) // 2
    pieces = (pl.ds(0, thick), pl.ds(thick, thick), pl.ds(2 * thick, thin), pl.ds(2 * thick + thin, thin))
    UP, DOWN, X, Y = range(4)
    target = {UP: up, DOWN: down, X: to_x, Y: to_y}

    def view(j, piece):
        return slots.at[j, pieces[piece], :]

    def pass_on(j, piece, way):
        remote(
            view(j, piece), view(j, piece), send.at[j, piece, way], recv.at[j, piece], (target[way], d)
        ).start()

    def arrived(j, piece):
        wait_for(view(j, piece), recv.at[j, piece])

    def sent(j, piece, way):
        wait_for(view(j, piece), send.at[j, piece, way])

    def spread(j):
        pass_on(j, 0, X)
        pass_on(j, 1, Y)
        pass_on(j, 0, Y)
        pass_on(j, 1, X)

    def go_up(j, which):
        @pl.when(has_up)
        def _():
            for piece in which:
                pass_on(j, piece, UP)

    def go_down(j, which):
        @pl.when(has_down)
        def _():
            for piece in which:
                pass_on(j, piece, DOWN)

    go_up(p, (0, 1))
    go_down(p, (0, 1))
    pass_on(p, 2, X)
    pass_on(p, 3, Y)
    spread(p)
    pass_on(p, 3, X)
    pass_on(p, 2, Y)
    go_up(p, (2, 3))
    go_down(p, (2, 3))

    gent[...] = gbo[d]
    for o in range(1, n_dim):
        wait_for(gbr.at[other(o)], e_recv.at[other(o)])
        gent[...] += gbr[other(o)]
    gent[0:width, :] += put(gq_re * r_re + gq_im * r_im, hot_lhs, 2)
    gent[wp : wp + width, :] += put(gq_im * r_re - gq_re * r_im, hot_lhs, 2)
    gent_copy = pltpu.make_async_copy(gent, gent_out, out_sem.at[0])
    gent_copy.start()
    g_re, g_im = gent[0:width, :], gent[wp : wp + width, :]
    esq[d] = jnp.sum(g_re * g_re, 0, keepdims=True) + jnp.sum(g_im * g_im, 0, keepdims=True)
    for o in range(1, n_dim):
        remote(esq.at[d], esq.at[d], eq_send.at[o], eq_recv.at[d], (p, other(o))).start()

    lanes = lax.broadcasted_iota(jnp.int32, (edges, PIECE), 1)

    def add_up(js, fresh):
        highs = []
        for k, j in enumerate(js):
            cut = slice(k * edges, (k + 1) * edges)
            high, low = split(slots[j], 2)
            batch[0:kp, cut] = high
            batch[kp : 2 * kp, cut] = low
            base, piece_of = low_high(slots[j, width : width + 1, :].astype(jnp.int32))
            down_rows = jnp.transpose(jnp.broadcast_to(base.astype(F32), (LANES, edges))).astype(jnp.int32)
            wide = jnp.concatenate([down_rows] * (PIECE // LANES), 1)
            hot_ref[cut, :] = jnp.where(lanes == wide, 1.0, 0.0).astype(BF16)
            highs.append(piece_of)
        highs = jnp.concatenate(highs, 1).astype(F32).astype(BF16)

        def body(c, carry):
            first = pl.multiple_of(c * PIECE, PIECE)
            here = highs == c.astype(F32).astype(BF16)
            mine = jnp.where(here, batch[...], jnp.zeros((), BF16))
            both = jnp.dot(mine, hot_ref[...], preferred_element_type=F32)
            total = both[0:kp] + both[kp : 2 * kp]
            if not fresh:
                total = total + acc[:, pl.ds(first, PIECE)]
            acc[:, pl.ds(first, PIECE)] = total
            return carry

        lax.fori_loop(0, rel_count // PIECE, body, 0)

    def cross(zz):
        from_x, from_y = index(zz, y, 1 - x), index(zz, 1 - y, x)
        arrived(from_x, 0)
        pass_on(from_x, 0, Y)
        arrived(from_y, 1)
        pass_on(from_y, 1, X)

    def plane():
        from_x, from_y, corner = index(z, y, 1 - x), index(z, 1 - y, x), index(z, 1 - y, 1 - x)
        arrived(from_x, 2)
        pass_on(from_x, 2, Y)
        arrived(from_y, 3)
        pass_on(from_y, 3, X)
        go_up(from_x, (2,))
        go_down(from_x, (2,))
        go_up(from_y, (3,))
        go_down(from_y, (3,))
        for j, piece in ((from_x, 3), (from_y, 2), (corner, 2), (corner, 3)):
            arrived(j, piece)
            go_up(j, (piece,))
            go_down(j, (piece,))

    def planes(k):
        below, above = z - k, z + k

        @pl.when(below >= 0)
        def _():
            for q in range(4):
                j = below * 4 + q
                for piece in (2, 3):
                    arrived(j, piece)
                    go_up(j, (piece,))

        @pl.when(above < deep)
        def _():
            for q in range(4):
                j = above * 4 + q
                for piece in (2, 3):
                    arrived(j, piece)
                    go_down(j, (piece,))

    def add_plane(zz, fresh):
        for yy, xx, which in ((y, 1 - x, (1,)), (1 - y, x, (0,)), (1 - y, 1 - x, (0, 1))):
            for piece in which:
                arrived(index(zz, yy, xx), piece)
        add_up([zz * 4 + q for q in range(4)], fresh)

    def add_planes(k):
        below, above = z - k, z + k

        @pl.when(below >= 0)
        def _():
            add_plane(below, False)

        @pl.when(above < deep)
        def _():
            add_plane(above, False)

    def column(k, carry):
        below, above = z - k, z + k

        @pl.when(below >= 0)
        def _():
            j = index(below, y, x)
            arrived(j, 0)
            arrived(j, 1)
            go_up(j, (0, 1))
            spread(j)

        @pl.when(above < deep)
        def _():
            j = index(above, y, x)
            arrived(j, 0)
            arrived(j, 1)
            go_down(j, (0, 1))
            spread(j)

        @pl.when(below + 1 >= 0)
        def _():
            cross(below + 1)

        @pl.when((above - 1 < deep) & (k > 1))
        def _():
            cross(above - 1)

        @pl.when(k == 1)
        def _():
            plane()

        @pl.when(k > 1)
        def _():
            planes(k - 1)

        @pl.when(k == 2)
        def _():
            add_plane(z, True)

        @pl.when(k > 2)
        def _():
            add_planes(k - 2)

        return carry

    lax.fori_loop(1, deep, column, 0)
    for far in (z - (deep - 1), z + (deep - 1)):

        @pl.when((far >= 0) & (far < deep))
        def _(far=far):
            cross(far)

    last = deep - 1
    if deep == 2:
        add_plane(z, True)
    if deep > 2:
        add_planes(last - 1)
    planes(last)
    add_planes(last)

    total = esq[d]
    for o in range(1, n_dim):
        wait_for(esq.at[other(o)], eq_recv.at[other(o)])
        total = total + esq[other(o)]
    ent_sq[...] = total

    acc_copy = pltpu.make_async_copy(acc, acc_out, out_sem.at[1])
    acc_copy.start()
    t_re, t_im = acc[0:width, :], acc[wp : wp + width, :]
    rsq[d] = jnp.sum(t_re * t_re, 0, keepdims=True) + jnp.sum(t_im * t_im, 0, keepdims=True)
    for o in range(1, n_dim):
        remote(rsq.at[d], rsq.at[d], rq_send.at[o], rq_recv.at[d], (p, other(o))).start()
    total = rsq[d]
    for o in range(1, n_dim):
        wait_for(rsq.at[other(o)], rq_recv.at[other(o)])
        total = total + rsq[other(o)]
    rel_sq[...] = total

    def drain(zz, carry):
        j = index(zz, y, x)

        @pl.when((zz <= z) & has_up)
        def _():
            sent(j, 0, UP)
            sent(j, 1, UP)
            for q in range(4):
                sent(zz * 4 + q, 2, UP)
                sent(zz * 4 + q, 3, UP)

        @pl.when((zz >= z) & has_down)
        def _():
            sent(j, 0, DOWN)
            sent(j, 1, DOWN)
            for q in range(4):
                sent(zz * 4 + q, 2, DOWN)
                sent(zz * 4 + q, 3, DOWN)

        for piece in (0, 1):
            sent(j, piece, X)
            sent(j, piece, Y)
        sent(index(zz, y, 1 - x), 0, Y)
        sent(index(zz, 1 - y, x), 1, X)
        return carry

    for piece in (2, 3):
        sent(p, piece, X)
        sent(p, piece, Y)
    sent(index(z, y, 1 - x), 2, Y)
    sent(index(z, 1 - y, x), 3, X)
    lax.fori_loop(0, deep, drain, 0)
    gent_copy.wait()
    acc_copy.wait()
    for o in range(1, n_dim):
        wait_for(bf.at[d], b_send.at[o])
        wait_for(gbo.at[d], e_send.at[o])
        wait_for(esq.at[d], eq_send.at[o])
        wait_for(rsq.at[d], rq_send.at[o])
    for i in range(units):
        s, g = unit(d, i)
        when(s != 0, lambda i=i: wait_for(mt.at[0], m_send.at[i]))
        when(s != 0, lambda i=i: wait_for(qs.at[0], q_send.at[i, 0]))
        when(s != 0, lambda i=i: wait_for(gqo.at[i, 0], g_send.at[i, 0]))
        for o in range(1, n_dim):
            wait_for(qs.at[0], q_send.at[i, o])
            wait_for(gqo.at[i, 0], g_send.at[i, o])


def update_kernel(
    gent, ent_sq, ent_re, ent_im, ent_acc, acc, rel_sq, rel_re, rel_im, rel_acc,
    new_re, new_im, new_acc, new_rre, new_rim, new_racc,
):
    width, wp = ent_re.shape[0], gent.shape[0] // 2
    for grad, sq, old_re, old_im, old, out_re, out_im, out in (
        (gent, ent_sq, ent_re, ent_im, ent_acc, new_re, new_im, new_acc),
        (acc, rel_sq, rel_re, rel_im, rel_acc, new_rre, new_rim, new_racc),
    ):
        total = old[...] + sq[...] / D
        out[...] = total
        scale = RATE / jnp.sqrt(total)
        out_re[...] = old_re[...] - scale * grad[0:width, :]
        out_im[...] = old_im[...] - scale * grad[wp : wp + width, :]


def per_device(
    n_dom, n_dim,
    ent_re, ent_im, ent_acc, rel_re, rel_im, rel_acc, lhs_rows, rhs_rows, rel_ids, neg_rows, bucket_step,
):
    width, rows = ent_re.shape
    rel_count = rel_re.shape[1]
    groups, per_edge = lhs_rows.shape
    wp = (width // 8 + 1) * 8
    kp = 2 * wp
    units = groups * STEPS // n_dim
    edges = groups * per_edge
    deep_k = n_dim * kp
    vmem = pl.BlockSpec(memory_space=pltpu.VMEM)
    hbm = pl.BlockSpec(memory_space=pl.ANY)
    dma = pltpu.SemaphoreType.DMA
    shape = jax.ShapeDtypeStruct
    args = (
        ent_re, ent_im, rel_re, rel_im,
        lhs_rows, rhs_rows, rel_ids, neg_rows, bucket_step.reshape(1, groups),
    )
    gent, ent_sq, acc, rel_sq = pl.pallas_call(
        functools.partial(round_kernel, n_dom, n_dim),
        out_shape=(
            shape((kp, rows), F32), shape((1, rows), F32), shape((kp, rel_count), F32), shape((1, rel_count), F32)
        ),
        in_specs=[hbm] * len(args),
        out_specs=(hbm, vmem, hbm, vmem),
        scratch_shapes=[pltpu.VMEM(a.shape, a.dtype) for a in args] + [
            pltpu.VMEM((groups, kp, per_edge), F32),
            pltpu.VMEM((units, n_dim, kp, per_edge), F32),
            pltpu.VMEM((groups, META, LANES), jnp.int32),
            pltpu.VMEM((units, META, LANES), jnp.int32),
            pltpu.VMEM((n_dim, kp, rows), F32),
            pltpu.VMEM((3, rows, deep_k), BF16),
            pltpu.VMEM((2, deep_k, rows), BF16),
            pltpu.VMEM((2, rows, units * per_edge), BF16),
            pltpu.VMEM((units, n_dim, kp, per_edge), F32),
            pltpu.VMEM((STEPS, groups, kp, per_edge), F32),
            pltpu.VMEM((n_dim, kp, rows), F32),
            pltpu.VMEM((n_dim, kp, rows), F32),
            pltpu.VMEM((kp, rows), F32),
            pltpu.VMEM((n_dom, kp, edges), F32),
            pltpu.VMEM((kp, rel_count), F32),
            pltpu.VMEM((2 * kp, 4 * edges), BF16),
            pltpu.VMEM((4 * edges, PIECE), BF16),
            pltpu.VMEM((n_dim, 1, rows), F32),
            pltpu.VMEM((n_dim, 1, rel_count), F32),
            dma((len(args),)), dma((2,)),
            dma((units, n_dim)), dma((units, n_dim)),
            dma((units,)), dma((units,)),
            dma((n_dim,)), dma((n_dim,)),
            dma((units, n_dim)), dma((STEPS, groups)),
            dma((n_dim,)), dma((n_dim,)),
            dma((n_dom, 4, 4)), dma((n_dom, 4)),
            dma((n_dim,)), dma((n_dim,)),
            dma((n_dim,)), dma((n_dim,)),
        ],
        compiler_params=pltpu.CompilerParams(
            collective_id=0, has_side_effects=True, vmem_limit_bytes=60 * 1024 * 1024
        ),
    )(*args)
    steps = rows // LANES
    ent, ent_row = pl.BlockSpec((width, LANES), lambda c: (0, c)), pl.BlockSpec((1, LANES), lambda c: (0, c))
    some = rel_count // steps
    rel, rel_row = pl.BlockSpec((width, some), lambda c: (0, c)), pl.BlockSpec((1, some), lambda c: (0, c))
    outs = pl.pallas_call(
        update_kernel,
        grid=(steps,),
        out_shape=tuple(shape(s, F32) for s in (
            (width, rows), (width, rows), (1, rows), (width, rel_count), (width, rel_count), (1, rel_count)
        )),
        in_specs=[
            pl.BlockSpec((kp, LANES), lambda c: (0, c)), ent_row, ent, ent, ent_row,
            pl.BlockSpec((kp, some), lambda c: (0, c)), rel_row, rel, rel, rel_row,
        ],
        out_specs=(ent, ent, ent_row, rel, rel, rel_row),
        compiler_params=pltpu.CompilerParams(vmem_limit_bytes=60 * 1024 * 1024),
    )(
        gent, ent_sq, ent_re, ent_im, ent_acc.reshape(1, rows),
        acc, rel_sq, rel_re, rel_im, rel_acc.reshape(1, rel_count),
    )
    return outs[0], outs[1], outs[2].reshape(rows), outs[3], outs[4], outs[5].reshape(rel_count)


def solution(mesh):
    return jax.shard_map(
        functools.partial(per_device, mesh.shape["dom"], mesh.shape["dim"]),
        mesh=mesh,
        in_specs=(
            P("dim", "dom"),
            P("dim", "dom"),
            P("dom"),
            P("dim", None),
            P("dim", None),
            P(),
            P("dom", None),
            P("dom", None),
            P("dom", None),
            P("dom", None),
            P("dom"),
        ),
        out_specs=(P("dim", "dom"), P("dim", "dom"), P("dom"), P("dim", None), P("dim", None), P()),
        check_vma=False,
    )
```

```python
import functools
import jax
import jax.numpy as jnp
from jax import lax
from jax.experimental import pallas as pl
from jax.experimental.pallas import tpu as pltpu
from jax.sharding import PartitionSpec as P

D = 400
STEPS = 4
RATE = 0.1
MESH = pl.DeviceIdType.MESH
F32 = jnp.float32
BF16 = jnp.bfloat16
META = 16
LANES = 128
PIECE = 256


def low_high(ids):
    high = lax.div(ids, PIECE)
    return ids - high * PIECE, high


def split(x, n):
    parts = []
    for _ in range(n):
        part = x.astype(BF16)
        parts.append(part)
        x = x - part.astype(F32)
    return parts


def one_hot(row, first, count):
    rows = lax.broadcasted_iota(jnp.int32, (count, row.shape[1]), 0) + first
    return jnp.where(rows == row, 1.0, 0.0).astype(BF16)


def pick(x, hot, n):
    total = None
    for part in split(x, n):
        term = jnp.dot(part, hot, preferred_element_type=F32)
        total = term if total is None else total + term
    return total


def put(x, hot, n):
    total = None
    for part in split(x, n):
        term = lax.dot_general(part, hot, (((1,), (1,)), ((), ())), preferred_element_type=F32)
        total = term if total is None else total + term
    return total


def when(pred, fn):
    if isinstance(pred, bool):
        if pred:
            fn()
    else:
        pl.when(pred)(fn)


def wait_for(ref, sem):
    pltpu.make_async_copy(ref, ref, sem).wait()


def remote(src, dst, send, recv, device):
    return pltpu.make_async_remote_copy(
        src_ref=src, dst_ref=dst, send_sem=send, recv_sem=recv, device_id=device, device_id_type=MESH
    )


def round_kernel(
    n_dom, n_dim,
    ent_re_in, ent_im_in, rel_re_in, rel_im_in, lhs_in, rhs_in, ids_in, neg_in, bs_in,
    gent_out, ent_sq, acc_out, rel_sq,
    ent_re, ent_im, rel_re, rel_im, lhs_ref, rhs_ref, ids_ref, neg_ref, bs_ref,
    qs, qr, mt, mr, bf, bt, bp, wts, gqo, gqr, gbo, gbr, gent,
    slots, acc, batch, hot_ref, esq, rsq,
    in_sem, out_sem,
    q_send, q_recv, m_send, m_recv, b_send, b_recv, g_send, g_recv, e_send, e_recv,
    send, recv, eq_send, eq_recv, rq_send, rq_recv,
):
    p, d = lax.axis_index("dom"), lax.axis_index("dim")
    width, rows = ent_re.shape
    groups, per_edge = lhs_ref.shape
    edges = groups * per_edge
    rel_count = rel_re.shape[1]
    kp = qs.shape[1]
    wp = kp // 2
    units = groups * STEPS // n_dim
    deep = n_dom // 4
    z, y, x = lax.div(p, 4), lax.rem(lax.div(p, 2), 2), lax.rem(p, 2)

    def index(zz, yy, xx):
        return zz * 4 + yy * 2 + xx

    def unit(td, i):
        if n_dim == groups:
            return i, td
        number = td + n_dim * i
        return lax.div(number, groups), lax.rem(number, groups)

    def holder(offset):
        return lax.rem(p + offset + n_dom, n_dom)

    def other(o):
        return lax.rem(d + o, n_dim)

    to_x, to_y = index(z, y, 1 - x), index(z, 1 - y, x)
    up, down = p + 4, p - 4
    has_up, has_down = z < deep - 1, z > 0

    barrier = pltpu.get_barrier_semaphore()

    def greet(dom, dim):
        pl.semaphore_signal(barrier, inc=1, device_id=(dom, dim), device_id_type=MESH)

    peers = 0
    for offset in range(1 - STEPS, STEPS):
        for o in range(n_dim):
            if offset != 0 or o != 0:
                greet(holder(offset), other(o))
                peers += 1
    greet(to_x, d)
    greet(to_y, d)

    @pl.when(has_up)
    def _():
        greet(up, d)

    @pl.when(has_down)
    def _():
        greet(down, d)

    fetches = []
    for k, (src, dst) in enumerate([
        (lhs_in, lhs_ref), (rhs_in, rhs_ref), (ids_in, ids_ref), (neg_in, neg_ref), (bs_in, bs_ref),
        (ent_re_in, ent_re), (ent_im_in, ent_im), (rel_re_in, rel_re), (rel_im_in, rel_im),
    ]):
        fetches.append(pltpu.make_async_copy(src, dst, in_sem.at[k]))
        fetches[-1].start()
    mt[...] = jnp.full(mt.shape, -1, jnp.int32)
    qs[...] = jnp.zeros(qs.shape, F32)
    slots[p] = jnp.zeros((kp, edges), F32)
    bf[d] = jnp.zeros((kp, rows), F32)
    for fetch in fetches[:7]:
        fetch.wait()

    n_neg = neg_ref.shape[1]
    for g in range(groups):
        for j in range(0, n_neg, LANES):
            wide = min(LANES, n_neg - j)
            mt[g, j // LANES : j // LANES + 1, 0:wide] = neg_ref[g : g + 1, j : j + wide]
        mt[g, 8:9, :] = rhs_ref[g : g + 1, :]
        mt[g, 9:10, :] = jnp.broadcast_to(bs_ref[:, g : g + 1], (1, LANES))
    bf[d, 0:width, :] = ent_re[...]
    bf[d, wp : wp + width, :] = ent_im[...]

    pl.semaphore_wait(barrier, peers + 2 + jnp.minimum(z, 1) + jnp.minimum(deep - 1 - z, 1))

    for i in range(units):
        s, g = unit(d, i)

        def local_meta(g=g, i=i):
            mr[i] = mt[g]

        def far_meta(s=s, g=g, i=i):
            remote(mt.at[g], mr.at[i], m_send.at[i], m_recv.at[i], (holder(-s), d)).start()

        when(s == 0, local_meta)
        when(s != 0, far_meta)
    for o in range(1, n_dim):
        remote(bf.at[d], bf.at[d], b_send.at[o], b_recv.at[d], (p, other(o))).start()

    lhs = jnp.concatenate([lhs_ref[g : g + 1, :] for g in range(groups)], 1)
    ids = jnp.concatenate([ids_ref[g : g + 1, :] for g in range(groups)], 1)
    hot_lhs = one_hot(lhs, 0, rows)
    h_re, h_im = pick(ent_re[...], hot_lhs, 3), pick(ent_im[...], hot_lhs, 3)
    for fetch in fetches[7:]:
        fetch.wait()
    base, high_of = low_high(ids)
    hot_ids = one_hot(base, 0, PIECE)

    def gather(c, carry):
        first = pl.multiple_of(c * PIECE, PIECE)
        here = high_of == c
        return (
            jnp.where(here, pick(rel_re[:, pl.ds(first, PIECE)], hot_ids, 3), carry[0]),
            jnp.where(here, pick(rel_im[:, pl.ds(first, PIECE)], hot_ids, 3), carry[1]),
        )

    empty = jnp.zeros((width, edges), F32)
    r_re, r_im = lax.fori_loop(0, rel_count // PIECE, gather, (empty, empty))
    q_re = h_re * r_re - h_im * r_im
    q_im = h_re * r_im + h_im * r_re
    for g in range(groups):
        part = slice(g * per_edge, (g + 1) * per_edge)
        qs[g, 0:width, :] = q_re[:, part]
        qs[g, wp : wp + width, :] = q_im[:, part]

    for i in reversed(range(units)):
        for o in range(n_dim):
            td = other(o)
            s, g = unit(td, i)

            def near_query(g=g, i=i):
                qr[i, d] = qs[g]

            def far_query(s=s, g=g, i=i, o=o, td=td):
                remote(qs.at[g], qr.at[i, d], q_send.at[i, o], q_recv.at[i, d], (holder(-s), td)).start()

            if o == 0:
                when(s == 0, near_query)
                when(s != 0, far_query)
            else:
                far_query()

    for o in range(1, n_dim):
        wait_for(bf.at[other(o)], b_recv.at[other(o)])
    deep_k = n_dim * kp
    block = bf[...].reshape(deep_k, rows)
    for k, part in enumerate(split(block, 2)):
        bp[k] = part
    for k, part in enumerate(split(jnp.transpose(block), 3)):
        bt[k] = part

    at = lax.broadcasted_iota(jnp.int32, (rows, per_edge), 0)
    ones = jnp.ones((LANES, per_edge), BF16)

    def dot(a, b):
        return jnp.dot(a, b, preferred_element_type=F32)

    for i in range(units):
        s, g = unit(d, i)
        when(s != 0, lambda i=i: wait_for(mr.at[i], m_recv.at[i]))
        hits = jnp.zeros((rows, LANES), F32)
        for j in range(8):
            hits = hits + jnp.where(at == mr[i, j : j + 1, :], 1.0, 0.0)
        cnt = dot(hits.astype(BF16), ones)
        hit = at == mr[i, 8:9, :]
        live = jnp.where(mr[i, 9:10, :] == s, 1.0, 0.0)
        for o in range(n_dim):
            if o == 0:
                when(s != 0, lambda i=i: wait_for(qr.at[i, d], q_recv.at[i, d]))
            else:
                wait_for(qr.at[i, other(o)], q_recv.at[i, other(o)])
        q0, q1, q2 = split(qr[i].reshape(deep_k, per_edge), 3)
        b0, b1, b2 = bt[0], bt[1], bt[2]
        st = dot(b0, q0) + (dot(b0, q1) + dot(b1, q0)) + (dot(b0, q2) + dot(b2, q0) + dot(b1, q1))
        pos = jnp.sum(jnp.where(hit, st, 0.0), 0, keepdims=True)
        masked = jnp.where(cnt > 0.0, st, -3.0e38)
        top = jnp.maximum(jnp.max(masked, 0, keepdims=True), pos)
        e_neg = cnt * jnp.exp(masked - top)
        e_pos = jnp.exp(pos - top)
        scale = live / (e_pos + jnp.sum(e_neg, 0, keepdims=True))
        w = e_neg * scale + jnp.where(hit, e_pos * scale - live, 0.0)
        w0, w1 = split(w, 2)
        wts[0, :, i * per_edge : (i + 1) * per_edge] = w0
        wts[1, :, i * per_edge : (i + 1) * per_edge] = w1
        gq = dot(bp[0], w0) + (dot(bp[0], w1) + dot(bp[1], w0))
        gqo[i] = gq.reshape(n_dim, kp, per_edge)
        for o in range(n_dim):
            td = other(o)

            def near_grad(s=s, g=g, i=i):
                gqr[s, g] = gqo[i, d]

            def far_grad(s=s, g=g, i=i, o=o, td=td):
                remote(gqo.at[i, td], gqr.at[s, g], g_send.at[i, o], g_recv.at[s, g], (holder(s), td)).start()

            if o == 0:
                when(s == 0, near_grad)
                when(s != 0, far_grad)
            else:
                far_grad()
    q = jnp.concatenate([qr[i].reshape(deep_k, per_edge) for i in range(units)], 1)
    q0, q1 = split(q, 2)
    turned = (((1,), (1,)), ((), ()))
    gb = lax.dot_general(q0, wts[0], turned, preferred_element_type=F32)
    gb = gb + lax.dot_general(q0, wts[1], turned, preferred_element_type=F32)
    gb = gb + lax.dot_general(q1, wts[0], turned, preferred_element_type=F32)
    gbo[...] = gb.reshape(n_dim, kp, rows)
    for o in range(1, n_dim):
        remote(gbo.at[other(o)], gbr.at[d], e_send.at[o], e_recv.at[d], (p, other(o))).start()

    cols = []
    for g in range(groups):
        total = None
        for s in range(STEPS):
            handler = (s * groups + g) % n_dim
            if s == 0:
                when(d != handler, lambda s=s, g=g: wait_for(gqr.at[s, g], g_recv.at[s, g]))
            else:
                wait_for(gqr.at[s, g], g_recv.at[s, g])
            total = gqr[s, g] if total is None else total + gqr[s, g]
        cols.append(total)
    gq = jnp.concatenate(cols, 1)
    gq_re, gq_im = gq[0:width], gq[wp : wp + width]
    slots[p, 0:width, :] = gq_re * h_re + gq_im * h_im
    slots[p, wp : wp + width, :] = gq_im * h_re - gq_re * h_im
    slots[p, width : width + 1, :] = ids.astype(F32)

    thin = max(1, (kp // 8 + 4) // 9) * 8
    thick = (kp - 2 * thin) // 2
    pieces = (pl.ds(0, thick), pl.ds(thick, thick), pl.ds(2 * thick, thin), pl.ds(2 * thick + thin, thin))
    UP, DOWN, X, Y = range(4)
    target = {UP: up, DOWN: down, X: to_x, Y: to_y}

    def view(j, piece):
        return slots.at[j, pieces[piece], :]

    def pass_on(j, piece, way):
        remote(
            view(j, piece), view(j, piece), send.at[j, piece, way], recv.at[j, piece], (target[way], d)
        ).start()

    def arrived(j, piece):
        wait_for(view(j, piece), recv.at[j, piece])

    def sent(j, piece, way):
        wait_for(view(j, piece), send.at[j, piece, way])

    def spread(j):
        pass_on(j, 0, X)
        pass_on(j, 1, Y)
        pass_on(j, 0, Y)
        pass_on(j, 1, X)

    def go_up(j, which):
        @pl.when(has_up)
        def _():
            for piece in which:
                pass_on(j, piece, UP)

    def go_down(j, which):
        @pl.when(has_down)
        def _():
            for piece in which:
                pass_on(j, piece, DOWN)

    go_up(p, (0, 1))
    go_down(p, (0, 1))
    pass_on(p, 2, X)
    pass_on(p, 3, Y)
    spread(p)
    pass_on(p, 3, X)
    pass_on(p, 2, Y)
    go_up(p, (2, 3))
    go_down(p, (2, 3))

    gent[...] = gbo[d]
    for o in range(1, n_dim):
        wait_for(gbr.at[other(o)], e_recv.at[other(o)])
        gent[...] += gbr[other(o)]
    gent[0:width, :] += put(gq_re * r_re + gq_im * r_im, hot_lhs, 2)
    gent[wp : wp + width, :] += put(gq_im * r_re - gq_re * r_im, hot_lhs, 2)
    gent_copy = pltpu.make_async_copy(gent, gent_out, out_sem.at[0])
    gent_copy.start()
    g_re, g_im = gent[0:width, :], gent[wp : wp + width, :]
    esq[d] = jnp.sum(g_re * g_re, 0, keepdims=True) + jnp.sum(g_im * g_im, 0, keepdims=True)
    for o in range(1, n_dim):
        remote(esq.at[d], esq.at[d], eq_send.at[o], eq_recv.at[d], (p, other(o))).start()

    lanes = lax.broadcasted_iota(jnp.int32, (edges, PIECE), 1)

    def add_up(js, fresh):
        highs = []
        for k, j in enumerate(js):
            cut = slice(k * edges, (k + 1) * edges)
            high, low = split(slots[j], 2)
            batch[0:kp, cut] = high
            batch[kp : 2 * kp, cut] = low
            base, piece_of = low_high(slots[j, width : width + 1, :].astype(jnp.int32))
            down_rows = jnp.transpose(jnp.broadcast_to(base.astype(F32), (LANES, edges))).astype(jnp.int32)
            wide = jnp.concatenate([down_rows] * (PIECE // LANES), 1)
            hot_ref[cut, :] = jnp.where(lanes == wide, 1.0, 0.0).astype(BF16)
            highs.append(piece_of)
        highs = jnp.concatenate(highs, 1).astype(F32).astype(BF16)

        def body(c, carry):
            first = pl.multiple_of(c * PIECE, PIECE)
            here = highs == c.astype(F32).astype(BF16)
            mine = jnp.where(here, batch[...], jnp.zeros((), BF16))
            both = jnp.dot(mine, hot_ref[...], preferred_element_type=F32)
            total = both[0:kp] + both[kp : 2 * kp]
            if not fresh:
                total = total + acc[:, pl.ds(first, PIECE)]
            acc[:, pl.ds(first, PIECE)] = total
            return carry

        lax.fori_loop(0, rel_count // PIECE, body, 0)

    def cross(zz):
        from_x, from_y = index(zz, y, 1 - x), index(zz, 1 - y, x)
        arrived(from_x, 0)
        pass_on(from_x, 0, Y)
        arrived(from_y, 1)
        pass_on(from_y, 1, X)

    def plane():
        from_x, from_y, corner = index(z, y, 1 - x), index(z, 1 - y, x), index(z, 1 - y, 1 - x)
        arrived(from_x, 2)
        pass_on(from_x, 2, Y)
        arrived(from_y, 3)
        pass_on(from_y, 3, X)
        go_up(from_x, (2,))
        go_down(from_x, (2,))
        go_up(from_y, (3,))
        go_down(from_y, (3,))
        for j, piece in ((from_x, 3), (from_y, 2), (corner, 2), (corner, 3)):
            arrived(j, piece)
            go_up(j, (piece,))
            go_down(j, (piece,))

    def planes(k):
        below, above = z - k, z + k

        @pl.when(below >= 0)
        def _():
            for q in range(4):
                j = below * 4 + q
                for piece in (2, 3):
                    arrived(j, piece)
                    go_up(j, (piece,))

        @pl.when(above < deep)
        def _():
            for q in range(4):
                j = above * 4 + q
                for piece in (2, 3):
                    arrived(j, piece)
                    go_down(j, (piece,))

    def add_plane(zz, fresh):
        for yy, xx, which in ((y, 1 - x, (1,)), (1 - y, x, (0,)), (1 - y, 1 - x, (0, 1))):
            for piece in which:
                arrived(index(zz, yy, xx), piece)
        add_up([zz * 4 + q for q in range(4)], fresh)

    def add_planes(k):
        below, above = z - k, z + k

        @pl.when(below >= 0)
        def _():
            add_plane(below, False)

        @pl.when(above < deep)
        def _():
            add_plane(above, False)

    def column(k, carry):
        below, above = z - k, z + k

        @pl.when(below >= 0)
        def _():
            j = index(below, y, x)
            arrived(j, 0)
            arrived(j, 1)
            go_up(j, (0, 1))
            spread(j)

        @pl.when(above < deep)
        def _():
            j = index(above, y, x)
            arrived(j, 0)
            arrived(j, 1)
            go_down(j, (0, 1))
            spread(j)

        @pl.when(below + 1 >= 0)
        def _():
            cross(below + 1)

        @pl.when((above - 1 < deep) & (k > 1))
        def _():
            cross(above - 1)

        @pl.when(k == 1)
        def _():
            plane()

        @pl.when(k > 1)
        def _():
            planes(k - 1)

        return carry

    lax.fori_loop(1, deep, column, 0)
    for far in (z - (deep - 1), z + (deep - 1)):

        @pl.when((far >= 0) & (far < deep))
        def _(far=far):
            cross(far)

    last = deep - 1
    add_plane(z, True)

    def nearer(k, carry):
        add_planes(k)
        return carry

    lax.fori_loop(1, last, nearer, 0)
    planes(last)
    add_planes(last)

    total = esq[d]
    for o in range(1, n_dim):
        wait_for(esq.at[other(o)], eq_recv.at[other(o)])
        total = total + esq[other(o)]
    ent_sq[...] = total

    acc_copy = pltpu.make_async_copy(acc, acc_out, out_sem.at[1])
    acc_copy.start()
    t_re, t_im = acc[0:width, :], acc[wp : wp + width, :]
    rsq[d] = jnp.sum(t_re * t_re, 0, keepdims=True) + jnp.sum(t_im * t_im, 0, keepdims=True)
    for o in range(1, n_dim):
        remote(rsq.at[d], rsq.at[d], rq_send.at[o], rq_recv.at[d], (p, other(o))).start()
    total = rsq[d]
    for o in range(1, n_dim):
        wait_for(rsq.at[other(o)], rq_recv.at[other(o)])
        total = total + rsq[other(o)]
    rel_sq[...] = total

    def drain(zz, carry):
        j = index(zz, y, x)

        @pl.when((zz <= z) & has_up)
        def _():
            sent(j, 0, UP)
            sent(j, 1, UP)
            for q in range(4):
                sent(zz * 4 + q, 2, UP)
                sent(zz * 4 + q, 3, UP)

        @pl.when((zz >= z) & has_down)
        def _():
            sent(j, 0, DOWN)
            sent(j, 1, DOWN)
            for q in range(4):
                sent(zz * 4 + q, 2, DOWN)
                sent(zz * 4 + q, 3, DOWN)

        for piece in (0, 1):
            sent(j, piece, X)
            sent(j, piece, Y)
        sent(index(zz, y, 1 - x), 0, Y)
        sent(index(zz, 1 - y, x), 1, X)
        return carry

    for piece in (2, 3):
        sent(p, piece, X)
        sent(p, piece, Y)
    sent(index(z, y, 1 - x), 2, Y)
    sent(index(z, 1 - y, x), 3, X)
    lax.fori_loop(0, deep, drain, 0)
    gent_copy.wait()
    acc_copy.wait()
    for o in range(1, n_dim):
        wait_for(bf.at[d], b_send.at[o])
        wait_for(gbo.at[d], e_send.at[o])
        wait_for(esq.at[d], eq_send.at[o])
        wait_for(rsq.at[d], rq_send.at[o])
    for i in range(units):
        s, g = unit(d, i)
        when(s != 0, lambda i=i: wait_for(mt.at[0], m_send.at[i]))
        when(s != 0, lambda i=i: wait_for(qs.at[0], q_send.at[i, 0]))
        when(s != 0, lambda i=i: wait_for(gqo.at[i, 0], g_send.at[i, 0]))
        for o in range(1, n_dim):
            wait_for(qs.at[0], q_send.at[i, o])
            wait_for(gqo.at[i, 0], g_send.at[i, o])


def update_kernel(
    gent, ent_sq, ent_re, ent_im, ent_acc, acc, rel_sq, rel_re, rel_im, rel_acc,
    new_re, new_im, new_acc, new_rre, new_rim, new_racc,
):
    width, wp = ent_re.shape[0], gent.shape[0] // 2
    for grad, sq, old_re, old_im, old, out_re, out_im, out in (
        (gent, ent_sq, ent_re, ent_im, ent_acc, new_re, new_im, new_acc),
        (acc, rel_sq, rel_re, rel_im, rel_acc, new_rre, new_rim, new_racc),
    ):
        total = old[...] + sq[...] / D
        out[...] = total
        scale = RATE / jnp.sqrt(total)
        out_re[...] = old_re[...] - scale * grad[0:width, :]
        out_im[...] = old_im[...] - scale * grad[wp : wp + width, :]


def per_device(
    n_dom, n_dim,
    ent_re, ent_im, ent_acc, rel_re, rel_im, rel_acc, lhs_rows, rhs_rows, rel_ids, neg_rows, bucket_step,
):
    width, rows = ent_re.shape
    rel_count = rel_re.shape[1]
    groups, per_edge = lhs_rows.shape
    wp = (width // 8 + 1) * 8
    kp = 2 * wp
    units = groups * STEPS // n_dim
    edges = groups * per_edge
    deep_k = n_dim * kp
    vmem = pl.BlockSpec(memory_space=pltpu.VMEM)
    hbm = pl.BlockSpec(memory_space=pl.ANY)
    dma = pltpu.SemaphoreType.DMA
    shape = jax.ShapeDtypeStruct
    args = (
        ent_re, ent_im, rel_re, rel_im,
        lhs_rows, rhs_rows, rel_ids, neg_rows, bucket_step.reshape(1, groups),
    )
    gent, ent_sq, acc, rel_sq = pl.pallas_call(
        functools.partial(round_kernel, n_dom, n_dim),
        out_shape=(
            shape((kp, rows), F32), shape((1, rows), F32), shape((kp, rel_count), F32), shape((1, rel_count), F32)
        ),
        in_specs=[hbm] * len(args),
        out_specs=(hbm, vmem, hbm, vmem),
        scratch_shapes=[pltpu.VMEM(a.shape, a.dtype) for a in args] + [
            pltpu.VMEM((groups, kp, per_edge), F32),
            pltpu.VMEM((units, n_dim, kp, per_edge), F32),
            pltpu.VMEM((groups, META, LANES), jnp.int32),
            pltpu.VMEM((units, META, LANES), jnp.int32),
            pltpu.VMEM((n_dim, kp, rows), F32),
            pltpu.VMEM((3, rows, deep_k), BF16),
            pltpu.VMEM((2, deep_k, rows), BF16),
            pltpu.VMEM((2, rows, units * per_edge), BF16),
            pltpu.VMEM((units, n_dim, kp, per_edge), F32),
            pltpu.VMEM((STEPS, groups, kp, per_edge), F32),
            pltpu.VMEM((n_dim, kp, rows), F32),
            pltpu.VMEM((n_dim, kp, rows), F32),
            pltpu.VMEM((kp, rows), F32),
            pltpu.VMEM((n_dom, kp, edges), F32),
            pltpu.VMEM((kp, rel_count), F32),
            pltpu.VMEM((2 * kp, 4 * edges), BF16),
            pltpu.VMEM((4 * edges, PIECE), BF16),
            pltpu.VMEM((n_dim, 1, rows), F32),
            pltpu.VMEM((n_dim, 1, rel_count), F32),
            dma((len(args),)), dma((2,)),
            dma((units, n_dim)), dma((units, n_dim)),
            dma((units,)), dma((units,)),
            dma((n_dim,)), dma((n_dim,)),
            dma((units, n_dim)), dma((STEPS, groups)),
            dma((n_dim,)), dma((n_dim,)),
            dma((n_dom, 4, 4)), dma((n_dom, 4)),
            dma((n_dim,)), dma((n_dim,)),
            dma((n_dim,)), dma((n_dim,)),
        ],
        compiler_params=pltpu.CompilerParams(
            collective_id=0, has_side_effects=True, vmem_limit_bytes=60 * 1024 * 1024
        ),
    )(*args)
    steps = 2 * (rows // LANES)
    ent, ent_row = pl.BlockSpec((width, LANES), lambda c: (0, c // 2)), pl.BlockSpec((1, LANES), lambda c: (0, c // 2))
    some = rel_count // steps
    rel, rel_row = pl.BlockSpec((width, some), lambda c: (0, c)), pl.BlockSpec((1, some), lambda c: (0, c))
    outs = pl.pallas_call(
        update_kernel,
        grid=(steps,),
        out_shape=tuple(shape(s, F32) for s in (
            (width, rows), (width, rows), (1, rows), (width, rel_count), (width, rel_count), (1, rel_count)
        )),
        in_specs=[
            pl.BlockSpec((kp, LANES), lambda c: (0, c // 2)), ent_row, ent, ent, ent_row,
            pl.BlockSpec((kp, some), lambda c: (0, c)), rel_row, rel, rel, rel_row,
        ],
        out_specs=(ent, ent, ent_row, rel, rel, rel_row),
        compiler_params=pltpu.CompilerParams(vmem_limit_bytes=60 * 1024 * 1024),
    )(
        gent, ent_sq, ent_re, ent_im, ent_acc.reshape(1, rows),
        acc, rel_sq, rel_re, rel_im, rel_acc.reshape(1, rel_count),
    )
    return outs[0], outs[1], outs[2].reshape(rows), outs[3], outs[4], outs[5].reshape(rel_count)


def solution(mesh):
    return jax.shard_map(
        functools.partial(per_device, mesh.shape["dom"], mesh.shape["dim"]),
        mesh=mesh,
        in_specs=(
            P("dim", "dom"),
            P("dim", "dom"),
            P("dom"),
            P("dim", None),
            P("dim", None),
            P(),
            P("dom", None),
            P("dom", None),
            P("dom", None),
            P("dom", None),
            P("dom"),
        ),
        out_specs=(P("dim", "dom"), P("dim", "dom"), P("dom"), P("dim", None), P("dim", None), P()),
        check_vma=False,
    )
```
